32 devices in a mesh: groups: 2 (over x), blk: 16 (over z, y, core).
Axes of the slice: x: 2, y: 2, z: 4, core: 2. Of those that a mesh axis runs over, the one named last changes fastest.
Arguments:
- embeddings: float32 [8192, 768], P(('groups', 'blk')), parts along dimension 0, may hold values from -6 to 6
- dest_pos: int32 [8192], P(('groups', 'blk')), parts along dimension 0, may hold values from 0 to 4095, as said below
- cluster_lengths: int32 [8], P('groups'), parts along dimension 0, may hold values from 1 to 2048, 4096 in all
- block_mask: int32 [32, 16], P('groups'), parts along dimension 0, may hold values 0 or 1
Outputs:
- top_cosine: float32 [8192], P(('groups', 'blk')), parts along dimension 0
- dup_direction: bfloat16 [8192, 768], P(('groups', 'blk')), parts along dimension 0
The draws below stay inside these ranges and needn't reach their ends.
There are 2 independent parts, one for each index of `groups`. The reference program is written for one: setup_inputs(seed, part) draws one part's arguments, and reference() takes and returns one part's arrays. A program takes and returns all parts, laid end to end along the dimension named above; each array names one. Nothing has to cross between parts.
Inputs may be any that keep to these rules, and one draw needn't show every extreme that they name: `dest_pos`: a permutation of the positions; at most 32 rows of one device's 256 rows have positions in one aligned block of 256 positions, and this bound is reached in every draw.
All inputs are finite; a program needn't handle non-finite values.
Results may differ from the reference program's by a relative error of at most 0.0055.
Values may be sent and summed in bfloat16 or wider, within the bound.
No kernel may reach another device: no remote copies, remote signals or barrier semaphores. Data moves between devices by JAX's collectives and lax.ppermute only.
A program may use at most 64 MiB of HBM per device.

```python
import math
import jax
import jax.numpy as jnp
import numpy as np
from jax import lax

D = 768
ROW_DEV = 256
NCLUST = 4
ROWS = 4096
N_BLK = 16


def draw_dest_pos(key, part):
    key = jax.random.fold_in(key, 11)
    count = ROWS // ROW_DEV
    share = ROW_DEV // count
    sigma = jax.random.permutation(jax.random.fold_in(key, 1), count)
    tau = jnp.roll(sigma, -1)
    source = jnp.arange(count)[:, None]
    counts = share + share * (source == sigma[None, :]).astype(jnp.int32) - share * (source == tau[None, :]).astype(jnp.int32)
    incl_src = jnp.cumsum(counts, axis=1)
    off_src = incl_src - counts
    off_dst = jnp.cumsum(counts, axis=0) - counts
    ranks = jnp.arange(ROW_DEV)
    target_dev = jnp.sum((incl_src[:, None, :] <= ranks[None, :, None]).astype(jnp.int32), axis=2)
    start_src = jnp.take_along_axis(off_src, target_dev, axis=1)
    start_dst = jnp.take_along_axis(off_dst, target_dev, axis=1)
    slot = start_dst + ranks[None, :] - start_src
    slot_perm = jax.vmap(lambda sub: jax.random.permutation(sub, ROW_DEV))(jax.random.split(jax.random.fold_in(key, 2), count))
    slot_final = slot_perm[target_dev, slot]
    target = target_dev * ROW_DEV + slot_final
    row_perm = jax.vmap(lambda sub: jax.random.permutation(sub, ROW_DEV))(jax.random.split(jax.random.fold_in(key, 3), count))
    result = jnp.zeros((count, ROW_DEV), jnp.int32).at[jnp.arange(count)[:, None], row_perm].set(target)
    return result.reshape(ROWS).astype(jnp.int32)


def with_ends(entries, key, smallest, largest):
    longest = entries.shape.index(max(entries.shape))
    spots = []
    for shift in (0, 1):
        where = [jax.random.randint(jax.random.fold_in(key, axis), (), 0, length) for axis, length in enumerate(entries.shape)]
        where[longest] = (where[longest] + shift) % entries.shape[longest]
        spots.append(tuple(where))
    return entries.at[spots[0]].set(smallest).at[spots[1]].set(largest)


def levels(rng, shape, shards, smallest, top_value):
    loudness = 1.0
    for dim, parts in shards:
        heights = jax.random.uniform(jax.random.fold_in(jax.random.fold_in(rng, 6), dim), (parts,), jnp.float32, smallest / len(shards), top_value / len(shards))
        loudness = loudness * jnp.repeat(jnp.exp(heights), shape[dim] // parts).reshape((-1,) + (1,) * (len(shape) - 1 - dim))
    return loudness


def length_profile(amount, total, reach, skew):
    weights = [(1 << 20) // math.isqrt(rank ** skew) + 1 for rank in range(2, amount + 1)]
    surplus, holding = total - reach - (amount - 1), [1] * (amount - 1)
    while surplus > 0:
        movable = [i for i in range(amount - 1) if holding[i] < reach]
        pool, budget = sum([weights[i] for i in movable]), surplus
        for i in movable:
            extra = min(reach - holding[i], max(1, budget * weights[i] // pool), surplus)
            holding[i] = holding[i] + extra
            surplus = surplus - extra
    return np.array([reach] + holding)


def uneven_parts(stream_key, count, total, bound, slope):
    if count == 2:
        one = jax.random.randint(stream_key, (), max(1, total - bound), min(bound, total - 1) + 1)
        return jnp.stack([one, total - one])
    lengths = jnp.asarray(length_profile(count, total, bound, slope), jnp.int32)
    couples = (count - 1) // 2
    donor, sink = lengths[1:1 + 2 * couples:2], lengths[2:2 + 2 * couples:2]
    room = jnp.minimum(donor - 1, bound - sink)
    passed = jax.random.randint(jax.random.fold_in(stream_key, 1), (couples,), 0, 1 << 20) % (room + 1)
    lengths = lengths.at[1:1 + 2 * couples:2].set(donor - passed).at[2:2 + 2 * couples:2].set(sink + passed)
    return lengths[jax.random.permutation(jax.random.fold_in(stream_key, 2), count)]


def bell_draw(rng, shape, spread, bound, cuts=(), held_as=jnp.bfloat16):
    entries = spread * jax.random.normal(rng, shape, jnp.float32)
    if cuts:
        entries = entries * levels(rng, shape, cuts, -0.22, 0.18)
    return jnp.clip(entries, -bound, bound).astype(held_as)


def setup_inputs(seed: int = 0, part: int = 0) -> dict:
    key_of = jax.random.split(jax.random.key(seed), 5)
    part_keys = jax.random.split(jax.random.fold_in(key_of[4], part), 5)
    return {
        "embeddings": bell_draw(part_keys[0], (ROWS, D), 1.0, 6.0, ((0, 16),), jnp.float32),
        "dest_pos": draw_dest_pos(jax.random.fold_in(jax.random.fold_in(key_of[4], part), 71), part),
        "cluster_lengths": uneven_parts(part_keys[2], NCLUST, ROWS, ROWS // 2, 2).astype(jnp.int32),
        "block_mask": with_ends((jax.random.randint(part_keys[3], (N_BLK, N_BLK), 0, 2) < 1).astype(jnp.int32), jax.random.fold_in(part_keys[3], 1), 0, 1),
    }


EPS = 1e-06
TEMP = 4.0

def cluster_of(positions, cluster_lengths):
    ends = jnp.cumsum(cluster_lengths).astype(jnp.int32)
    return lax.optimization_barrier(jnp.sum((positions[:, None] >= ends[None, :-1]).astype(jnp.int32), axis=1))

def reference(embeddings, dest_pos, cluster_lengths, block_mask):
    normed = embeddings * lax.rsqrt(lax.optimization_barrier(jnp.sum(embeddings * embeddings, axis=1, keepdims=True)) + EPS)
    unit = normed.astype(jnp.bfloat16)
    ordered = jnp.zeros((ROWS, D), jnp.bfloat16).at[dest_pos].set(unit)
    positions = jnp.arange(ROWS, dtype=jnp.int32)
    clusters = cluster_of(positions, cluster_lengths)
    blocks = positions // ROW_DEV

    def per_block(index):
        start = (index * ROW_DEV).astype(jnp.int32)
        query = lax.dynamic_slice_in_dim(ordered, start, ROW_DEV, 0)
        query_pos = start + jnp.arange(ROW_DEV, dtype=jnp.int32)
        query_cl = lax.dynamic_slice_in_dim(clusters, start, ROW_DEV, 0)
        scores = lax.dot_general(query, ordered, (((1,), (1,)), ((), ())), preferred_element_type=jnp.float32)
        same = query_cl[:, None] == clusters[None, :]
        earlier = same & (positions[None, :] < query_pos[:, None])
        top = lax.optimization_barrier(jnp.max(jnp.where(earlier, scores, jnp.float32(-1.0)), axis=1))
        mask_row = block_mask[index][blocks]
        allowed = same & ((mask_row[None, :] == 1) | (positions[None, :] == query_pos[:, None]))
        weights = jnp.where(allowed, jnp.exp(TEMP * scores), jnp.float32(0.0)).astype(jnp.bfloat16)
        total = jnp.dot(weights, ordered, preferred_element_type=jnp.float32)
        scale = jnp.sqrt(jnp.float32(D)) * lax.rsqrt(lax.optimization_barrier(jnp.sum(total * total, axis=1, keepdims=True)) + EPS)
        return (top, (total * scale).astype(jnp.bfloat16))
    tops, dirs = lax.map(per_block, jnp.arange(ROWS // ROW_DEV, dtype=jnp.int32))
    top_sorted = tops.reshape(ROWS)
    dir_sorted = dirs.reshape(ROWS, D)
    return (top_sorted[dest_pos], dir_sorted[dest_pos])
```

```python
import functools
import math

import jax
import jax.numpy as jnp
from jax import lax
from jax.experimental import pallas as pl
from jax.experimental.pallas import tpu as pltpu
from jax.sharding import PartitionSpec as P

EPS = 1e-06
TEMP = 4.0
LANES = 128
SPLIT = 128.0
TAIL = 8
VMEM_LIMIT = 48 * 1024 * 1024


def ring_order(chips):
    if chips <= 8:
        return list(range(0, chips, 2)) + list(range(1, chips, 2))[::-1]
    return list(range(chips))


def ring_perm(count, shift):
    order = ring_order(count // 2)
    pairs = []
    for at, chip in enumerate(order):
        to = order[(at + shift) % len(order)]
        pairs += [(2 * chip + core, 2 * to + core) for core in range(2)]
    return pairs


def call(body, out_shape, in_specs, flops, nbytes):
    many = isinstance(out_shape, (tuple, list))
    vmem = pl.BlockSpec(memory_space=pltpu.VMEM)
    return pl.pallas_call(
        body,
        out_shape=out_shape,
        in_specs=in_specs,
        out_specs=[vmem] * len(out_shape) if many else vmem,
        compiler_params=pltpu.CompilerParams(vmem_limit_bytes=VMEM_LIMIT),
        cost_estimate=pl.CostEstimate(flops=flops, bytes_accessed=nbytes, transcendentals=0),
    )


VM = pl.BlockSpec(memory_space=pltpu.VMEM)
SM = pl.BlockSpec(memory_space=pltpu.SMEM)


def prep_body(emb_ref, pos_ref, a_ref, b_ref, ah_ref, bh_ref):
    half = ah_ref.shape[0]
    pos = pos_ref[...].astype(jnp.float32)
    high = jnp.floor(pos * (1.0 / SPLIT))
    low = pos - high * SPLIT
    width = emb_ref.shape[1]
    row = jnp.concatenate(
        [high[0:1], low[0:1], high[1:2], low[1:2], jnp.zeros((1, width - 4 * half), jnp.float32)],
        axis=1,
    )
    tail = jnp.broadcast_to(row, (TAIL, width)).astype(jnp.bfloat16)
    for at, whole, alone in ((0, a_ref, ah_ref), (half, b_ref, bh_ref)):
        emb = emb_ref[at : at + half, :]
        unit = emb * lax.rsqrt(jnp.sum(emb * emb, axis=1, keepdims=True) + EPS)
        unit = unit.astype(jnp.bfloat16)
        alone[...] = unit
        whole[...] = jnp.concatenate([unit, tail], axis=0)


def rows_of(ref, half):
    return ref[...][:half]


def positions_of(ref, half):
    tail = ref[...][half:].astype(jnp.float32)
    return [
        tail[0:1, 2 * i * half : (2 * i + 1) * half] * SPLIT
        + tail[0:1, (2 * i + 1) * half : (2 * i + 2) * half]
        for i in range(2)
    ]


def column(row):
    size = row.shape[1]
    eye = lax.broadcasted_iota(jnp.int32, (size, size), 0) == lax.broadcasted_iota(
        jnp.int32, (size, size), 1
    )
    return jnp.sum(jnp.where(eye, row, 0.0), axis=1, keepdims=True)


def cluster_parts(pos, ends, clusters):
    index = jnp.zeros(pos.shape, jnp.int32)
    start = jnp.zeros(pos.shape, jnp.float32)
    for c in range(clusters - 1):
        past = pos >= ends[c]
        index = index + past.astype(jnp.int32)
        start = jnp.where(past, ends[c], start)
    return index, start


def ends_of(len_ref, clusters):
    ends, total = [], jnp.int32(0)
    for c in range(clusters - 1):
        total = total + len_ref[c]
        ends.append(total.astype(jnp.float32))
    return ends


def attend(
    rows, query, pos_b, start_b, feat, acc, top, keys, key_pos, ends, clusters, diagonal
):
    index, _ = cluster_parts(key_pos, ends, clusters)
    block = jnp.floor(key_pos * (1.0 / rows)).astype(jnp.int32)
    wanted = block * clusters + index
    size = key_pos.shape[1]
    onehot = (
        lax.broadcasted_iota(jnp.int32, (feat.shape[1], size), 0) == wanted
    ).astype(jnp.bfloat16)
    allowed = jnp.dot(feat, onehot, preferred_element_type=jnp.float32)
    scores = lax.dot_general(
        query, keys, (((1,), (1,)), ((), ())), preferred_element_type=jnp.float32
    )
    weights = []
    for at in range(0, size, LANES):
        part = scores[:, at : at + LANES]
        pos = key_pos[:, at : at + LANES]
        earlier = (pos < pos_b) & (pos >= start_b)
        top = jnp.maximum(top, jnp.where(earlier, part, -1.0))
        weight = jnp.exp2(part * (TEMP * math.log2(math.e)))
        masked = weight * allowed[:, at : at + LANES]
        if diagonal:
            masked = jnp.where(pos == pos_b, weight, masked)
        weights.append(masked.astype(jnp.bfloat16))
    acc = acc + jnp.dot(
        jnp.concatenate(weights, axis=1), keys, preferred_element_type=jnp.float32
    )
    return acc, top


def first_body(half, clusters, len_ref, mask_ref, a_ref, b_ref, sa_ref, sb_ref,
               acc_ref, top_ref, info_ref, feat_ref):
    ends = ends_of(len_ref, clusters)
    own = positions_of(a_ref, half)
    sib = positions_of(sa_ref, half)
    pos = jnp.concatenate([column(r) for r in own + sib], axis=0)
    index, start = cluster_parts(pos, ends, clusters)
    count = mask_ref.shape[0]
    block = jnp.floor(pos * (1.0 / (2 * half))).astype(jnp.int32)
    total = pos.shape[0]
    onehot = (block == lax.broadcasted_iota(jnp.int32, (total, count), 1)).astype(jnp.bfloat16)
    wide = count * clusters
    spread = (
        lax.broadcasted_iota(jnp.int32, (count, wide), 1) // clusters
        == lax.broadcasted_iota(jnp.int32, (count, wide), 0)
    ).astype(jnp.bfloat16)
    picked = jnp.dot(
        onehot, mask_ref[...].astype(jnp.bfloat16), preferred_element_type=jnp.float32
    ).astype(jnp.bfloat16)
    picked = jnp.dot(picked, spread, preferred_element_type=jnp.float32)
    lane_cluster = lax.broadcasted_iota(jnp.int32, (total, wide), 1) % clusters
    feat = jnp.where(lane_cluster == index, picked, 0.0).astype(jnp.bfloat16)
    feat_ref[...] = feat
    pos_b = jnp.broadcast_to(pos, (total, LANES))
    start_b = jnp.broadcast_to(start, (total, LANES))
    info_ref[0] = pos_b
    info_ref[1] = start_b
    query = jnp.concatenate([rows_of(r, half) for r in (a_ref, b_ref, sa_ref, sb_ref)], axis=0)
    acc, top = attend(
        2 * half, query, pos_b, start_b, feat,
        jnp.zeros((total, query.shape[1]), jnp.float32),
        jnp.full((total, LANES), -1.0, jnp.float32),
        query[: 2 * half], jnp.concatenate(own, axis=1), ends, clusters, True,
    )
    acc_ref[...] = acc
    top_ref[...] = top


def middle_body(half, clusters, groups, *refs):
    len_ref, info_ref, feat_ref, a_ref, b_ref, sa_ref, sb_ref, acc_in, top_in = refs[:9]
    key_refs = refs[9:-2]
    acc_ref, top_ref = refs[-2:]
    ends = ends_of(len_ref, clusters)
    query = jnp.concatenate([rows_of(r, half) for r in (a_ref, b_ref, sa_ref, sb_ref)], axis=0)
    acc, top = acc_in[...], top_in[...]
    for keys, pos in gather_keys(key_refs, groups, half):
        acc, top = attend(
            2 * half, query, info_ref[0], info_ref[1], feat_ref[...], acc, top, keys, pos,
            ends, clusters, False,
        )
    acc_ref[...] = acc
    top_ref[...] = top


def gather_keys(key_refs, groups, half):
    out = []
    for group in groups:
        keys = jnp.concatenate([rows_of(key_refs[r], half) for r, _, _ in group], axis=0)
        pos = jnp.concatenate(
            [positions_of(key_refs[p], half)[w] for _, p, w in group], axis=1
        )
        out.append((keys, pos))
    return out


def last_body(half, clusters, groups, *refs):
    len_ref, info_ref, feat_ref, a_ref, b_ref, acc_in, top_in, racc, rtop = refs[:9]
    key_refs = refs[9:-2]
    dir_ref, out_top = refs[-2:]
    ends = ends_of(len_ref, clusters)
    rows = 2 * half
    query = jnp.concatenate([rows_of(r, half) for r in (a_ref, b_ref)], axis=0)
    acc = acc_in[:rows] + racc[...]
    top = jnp.maximum(top_in[:rows], rtop[...])
    for keys, pos in gather_keys(key_refs, groups, half):
        acc, top = attend(
            2 * half, query, info_ref[0, :rows], info_ref[1, :rows], feat_ref[:rows], acc, top, keys, pos,
            ends, clusters, False,
        )
    width = acc.shape[1]
    scale = math.sqrt(width) * lax.rsqrt(jnp.sum(acc * acc, axis=1, keepdims=True) + EPS)
    dir_ref[...] = (acc * scale).astype(jnp.bfloat16)
    best = jnp.max(top, axis=1, keepdims=True)
    eye = lax.broadcasted_iota(jnp.int32, (half, half), 0) == lax.broadcasted_iota(
        jnp.int32, (half, half), 1
    )
    lines = [
        jnp.max(jnp.where(eye, best[at : at + half], -1.0), axis=0, keepdims=True)
        for at in (0, half)
    ]
    out_top[...] = jnp.concatenate(lines, axis=0)


def per_device(embeddings, dest_pos, cluster_lengths, block_mask):
    rows, width = embeddings.shape
    half = rows // 2
    count = lax.axis_size("blk")
    clusters = cluster_lengths.shape[0]
    chips = count // 2
    ahead, back = ring_perm(count, 1), ring_perm(count, -1)
    sibling = [(i, i ^ 1) for i in range(count)]

    def move(x, perm):
        return lax.ppermute(x, "blk", perm)

    def bf(n):
        return jax.ShapeDtypeStruct((n, width), jnp.bfloat16)

    def f32(*s):
        return jax.ShapeDtypeStruct(s, jnp.float32)

    full = half + TAIL
    a, b, ah, bh = call(
        prep_body, [bf(full), bf(full), bf(half), bf(half)], [VM, VM], rows * width * 4,
        rows * width * 8,
    )(embeddings, dest_pos.reshape(2, half))

    lead_f, lead_b, follow_f, follow_b = a, b, bh, ah
    rounds = []
    for step in range(chips // 2):
        lead_f, lead_b = move(lead_f, ahead), move(lead_b, back)
        if step < chips // 2 - 1:
            follow_f, follow_b = move(follow_f, ahead), move(follow_b, back)
            rounds.append((lead_f, lead_b, follow_f, follow_b))
        else:
            rounds.append((lead_f, lead_b))

    sa, sb = move(a, sibling), move(b, sibling)
    total = 2 * rows
    wide = count * clusters

    acc, top, info, feat = call(
        functools.partial(first_body, half, clusters),
        [f32(total, width), f32(total, LANES), f32(2, total, LANES),
         jax.ShapeDtypeStruct((total, wide), jnp.bfloat16)],
        [SM] + [VM] * 5, 4 * total * rows * width, 4 * 2**20,
    )(cluster_lengths, block_mask, a, b, sa, sb)

    pair = ((0, 0, 0), (1, 1, 1))

    def middle(acc, top, keys, groups):
        n = sum(len(g) for g in groups)
        return call(
            functools.partial(middle_body, half, clusters, groups),
            [f32(total, width), f32(total, LANES)],
            [SM] + [VM] * (8 + len(keys)), 4 * total * half * n * width, 5 * 2**20,
        )(cluster_lengths, info, feat, a, b, sa, sb, acc, top, *keys)

    for step in range(chips // 2 - 1):
        lf, lb = rounds[step][:2]
        if step == 0:
            acc, top = middle(acc, top, (lf, lb), (((0, 0, 0), (1, 1, 1)),))
        else:
            plf, plb, pff, pfb = rounds[step - 1]
            acc, top = middle(
                acc, top, (lf, lb, pff, pfb, plf, plb),
                (((0, 0, 0), (1, 1, 1)), ((2, 4, 1), (3, 5, 0))),
            )
    racc, rtop = move(acc[rows:], sibling), move(top[rows:], sibling)
    plf, plb, pff, pfb = rounds[-2]
    lf, lb = rounds[-1]
    late = [lf, lb, pff, pfb]
    others = [move(x, sibling) for x in late]
    splf, splb = move(plf, sibling), move(plb, sibling)
    keys = late + [plf, plb] + others + [splf, splb]
    groups = (
        ((2, 4, 1), (3, 5, 0)),
        ((8, 10, 1), (9, 11, 0)),
        ((0, 0, 0), (1, 1, 1)),
        ((6, 6, 0), (7, 7, 1)),
    )
    out_dir, out_top = call(
        functools.partial(last_body, half, clusters, groups),
        [jax.ShapeDtypeStruct((rows, width), jnp.bfloat16), f32(2, half)],
        [SM] + [VM] * (8 + len(keys)), 4 * rows * 8 * half * width, 5 * 2**20,
    )(cluster_lengths, info, feat, a, b, acc, top, racc, rtop, *keys)
    return out_top.reshape(rows), out_dir


def solution(mesh):
    placed = (P(("groups", "blk"), None), P(("groups", "blk")), P("groups"), P("groups", None))
    return jax.shard_map(
        per_device,
        mesh=mesh,
        in_specs=placed,
        out_specs=(P(("groups", "blk")), P(("groups", "blk"), None)),
        check_vma=False,
    )
```

```python
import functools
import math

import jax
import jax.numpy as jnp
from jax import lax
from jax.experimental import pallas as pl
from jax.experimental.pallas import tpu as pltpu
from jax.sharding import PartitionSpec as P

EPS = 1e-06
TEMP = 4.0
LANES = 128
SPLIT = 128.0
TAIL = 8
VMEM_LIMIT = 16 * 1024 * 1024
WEIGHT = 20


def ring_order(chips):
    if chips <= 8:
        return list(range(0, chips, 2)) + list(range(1, chips, 2))[::-1]
    return list(range(chips))


def ring_perm(count, shift):
    order = ring_order(count // 2)
    pairs = []
    for at, chip in enumerate(order):
        to = order[(at + shift) % len(order)]
        pairs += [(2 * chip + core, 2 * to + core) for core in range(2)]
    return pairs


VM = pl.BlockSpec(memory_space=pltpu.VMEM)
SM = pl.BlockSpec(memory_space=pltpu.SMEM)
HB = pl.BlockSpec(memory_space=pltpu.HBM)


def call(body, out_shape, in_specs, flops=1, out_specs=None, scratch=(), aliases=None,
         limit=VMEM_LIMIT):
    return pl.pallas_call(
        body,
        out_shape=out_shape,
        in_specs=in_specs,
        out_specs=out_specs or [VM] * len(out_shape),
        scratch_shapes=list(scratch),
        input_output_aliases=aliases or {},
        compiler_params=pltpu.CompilerParams(vmem_limit_bytes=limit),
        cost_estimate=pl.CostEstimate(flops=flops, bytes_accessed=1, transcendentals=0),
    )


def prep_body(emb_ref, pos_ref, a_ref, b_ref, ah_ref, bh_ref):
    half = ah_ref.shape[0]
    width = emb_ref.shape[1]
    pos = pos_ref[...]
    high = jnp.floor(pos * (1.0 / SPLIT))
    low = pos - high * SPLIT
    row = jnp.concatenate(
        [high[0:1], low[0:1], high[1:2], low[1:2], jnp.zeros((1, width - 4 * half), jnp.float32)],
        axis=1,
    )
    tail = jnp.broadcast_to(row, (TAIL, width)).astype(jnp.bfloat16)
    for i, whole, alone in ((0, a_ref, ah_ref), (1, b_ref, bh_ref)):
        emb = emb_ref[i * half : (i + 1) * half, :]
        unit = emb * lax.rsqrt(jnp.sum(emb * emb, axis=1, keepdims=True) + EPS)
        unit = unit.astype(jnp.bfloat16)
        alone[...] = unit
        whole[...] = jnp.concatenate([unit, tail], axis=0)


def rows_of(ref, half):
    return ref[...][:half]


def positions_of(ref, half):
    tail = ref[...][half:].astype(jnp.float32)
    return [
        tail[0:1, 2 * i * half : (2 * i + 1) * half] * SPLIT
        + tail[0:1, (2 * i + 1) * half : (2 * i + 2) * half]
        for i in range(2)
    ]


def column(row):
    size = row.shape[1]
    eye = lax.broadcasted_iota(jnp.int32, (size, size), 0) == lax.broadcasted_iota(
        jnp.int32, (size, size), 1
    )
    return jnp.sum(jnp.where(eye, row, 0.0), axis=1, keepdims=True)


def cluster_parts(pos, ends, clusters):
    index = jnp.zeros(pos.shape, jnp.int32)
    start = jnp.zeros(pos.shape, jnp.float32)
    for c in range(clusters - 1):
        past = pos >= ends[c]
        index = index + past.astype(jnp.int32)
        start = jnp.where(past, ends[c], start)
    return index, start


def ends_of(len_ref, clusters):
    ends, total = [], jnp.int32(0)
    for c in range(clusters - 1):
        total = total + len_ref[c]
        ends.append(total.astype(jnp.float32))
    return ends


def attend(
    rows, query, pos_b, start_b, feat, acc, top, keys, key_pos, ends, clusters, diagonal
):
    index, _ = cluster_parts(key_pos, ends, clusters)
    block = jnp.floor(key_pos * (1.0 / rows)).astype(jnp.int32)
    wanted = block * clusters + index
    size = key_pos.shape[1]
    onehot = (
        lax.broadcasted_iota(jnp.int32, (feat.shape[1], size), 0) == wanted
    ).astype(jnp.bfloat16)
    allowed = jnp.dot(feat, onehot, preferred_element_type=jnp.float32)
    scores = lax.dot_general(
        query, keys, (((1,), (1,)), ((), ())), preferred_element_type=jnp.float32
    )
    weights = []
    for at in range(0, size, LANES):
        part = scores[:, at : at + LANES]
        pos = key_pos[:, at : at + LANES]
        earlier = (pos < pos_b) & (pos >= start_b)
        top = jnp.maximum(top, jnp.where(earlier, part, -1.0))
        weight = jnp.exp2(part * (TEMP * math.log2(math.e)))
        masked = weight * allowed[:, at : at + LANES]
        if diagonal:
            masked = jnp.where(pos == pos_b, weight, masked)
        weights.append(masked.astype(jnp.bfloat16))
    acc = acc + jnp.dot(
        jnp.concatenate(weights, axis=1), keys, preferred_element_type=jnp.float32
    )
    return acc, top


def fold(rows, width, state, out_ref, query, info, feat, blocks, ends, clusters, diagonal=False):
    acc, top = state[:, :width], state[:, width:]
    for i, (keys, pos) in enumerate(blocks):
        acc, top = attend(
            rows, query, info[0], info[1], feat, acc, top, keys, pos, ends, clusters,
            diagonal and i == 0,
        )
    out_ref[:rows, :width] = acc
    out_ref[:rows, width:] = top


def first_body(half, clusters, len_ref, mask_hbm, a_ref, b_ref, sa_ref, sb_ref,
               f_ref, g_ref, own_ref, sib_ref, info_ref, feat_ref, mask_ref, sem):
    fetch = pltpu.make_async_copy(mask_hbm, mask_ref, sem.at[0])
    fetch.start()
    ends = ends_of(len_ref, clusters)
    own = positions_of(a_ref, half)
    sib = positions_of(sa_ref, half)
    pos = jnp.concatenate([column(r) for r in own + sib], axis=0)
    index, start = cluster_parts(pos, ends, clusters)
    count = mask_ref.shape[0]
    rows = 2 * half
    width = a_ref.shape[1]
    block = jnp.floor(pos * (1.0 / rows)).astype(jnp.int32)
    total = pos.shape[0]
    onehot = (block == lax.broadcasted_iota(jnp.int32, (total, count), 1)).astype(jnp.bfloat16)
    wide = count * clusters
    spread = (
        lax.broadcasted_iota(jnp.int32, (count, wide), 1) // clusters
        == lax.broadcasted_iota(jnp.int32, (count, wide), 0)
    ).astype(jnp.bfloat16)
    fetch.wait()
    picked = jnp.dot(
        onehot, mask_ref[...].astype(jnp.bfloat16), preferred_element_type=jnp.float32
    ).astype(jnp.bfloat16)
    picked = jnp.dot(picked, spread, preferred_element_type=jnp.float32)
    lane_cluster = lax.broadcasted_iota(jnp.int32, (total, wide), 1) % clusters
    feat = jnp.where(lane_cluster == index, picked, 0.0).astype(jnp.bfloat16)
    feat_ref[...] = feat
    info_ref[0] = jnp.broadcast_to(pos, (total, LANES))
    info_ref[1] = jnp.broadcast_to(start, (total, LANES))
    keys = jnp.concatenate([rows_of(r, half) for r in (a_ref, b_ref)], axis=0)
    blocks = [(keys, jnp.concatenate(own, axis=1))]
    blocks += gather_keys((f_ref, g_ref), (((0, 0, 0), (1, 1, 1)),), half)
    state = jnp.concatenate(
        [jnp.zeros((rows, width), jnp.float32), jnp.full((rows, LANES), -1.0, jnp.float32)],
        axis=1,
    )
    fold(rows, width, state, own_ref, keys, info_ref[:, :rows], feat[:rows], blocks, ends,
         clusters, True)
    other = jnp.concatenate([rows_of(r, half) for r in (sa_ref, sb_ref)], axis=0)
    fold(rows, width, state, sib_ref, other, info_ref[:, rows:], feat[rows:], blocks, ends,
         clusters)


def gather_keys(key_refs, groups, half):
    out = []
    for group in groups:
        keys = jnp.concatenate([rows_of(key_refs[r], half) for r, _, _ in group], axis=0)
        pos = jnp.concatenate(
            [positions_of(key_refs[p], half)[w] for _, p, w in group], axis=1
        )
        out.append((keys, pos))
    return out


def middle_body(half, clusters, groups, len_ref, info_ref, feat_ref, a_ref, b_ref, sa_ref,
                sb_ref, own_in, sib_in, *refs):
    key_refs, (own_ref, sib_ref) = refs[:-2], refs[-2:]
    ends = ends_of(len_ref, clusters)
    rows, width = 2 * half, a_ref.shape[1]
    blocks = gather_keys(key_refs, groups, half)
    for i, state_in, state_out, pair in (
        (0, own_in, own_ref, (a_ref, b_ref)), (1, sib_in, sib_ref, (sa_ref, sb_ref))
    ):
        query = jnp.concatenate([rows_of(r, half) for r in pair], axis=0)
        part = slice(i * rows, (i + 1) * rows)
        fold(rows, width, state_in[...], state_out, query, info_ref[:, part], feat_ref[part],
             blocks, ends, clusters)


def late_body(half, clusters, len_ref, info_ref, feat_ref, a_ref, b_ref, own_in, *refs):
    key_refs, own_ref = refs[:-1], refs[-1]
    ends = ends_of(len_ref, clusters)
    rows, width = 2 * half, a_ref.shape[1]
    blocks = gather_keys(key_refs, (((0, 0, 0), (1, 1, 1)),), half)
    query = jnp.concatenate([rows_of(r, half) for r in (a_ref, b_ref)], axis=0)
    fold(rows, width, own_in[...], own_ref, query, info_ref[:, :rows], feat_ref[:rows],
         blocks, ends, clusters)


def last_body(half, clusters, groups, len_ref, info_ref, feat_ref, a_ref, b_ref, own_in, got_ref,
              *refs):
    key_refs, (dir_ref, out_top) = refs[:-2], refs[-2:]
    ends = ends_of(len_ref, clusters)
    rows, width = 2 * half, a_ref.shape[1]
    query = jnp.concatenate([rows_of(r, half) for r in (a_ref, b_ref)], axis=0)
    acc = own_in[:, :width] + got_ref[:, :width]
    top = jnp.maximum(own_in[:, width:], got_ref[:, width:])
    for keys, pos in gather_keys(key_refs, groups, half):
        acc, top = attend(
            rows, query, info_ref[0, :rows], info_ref[1, :rows], feat_ref[:rows], acc, top, keys,
            pos, ends, clusters, False,
        )
    scale = math.sqrt(width) * lax.rsqrt(jnp.sum(acc * acc, axis=1, keepdims=True) + EPS)
    dir_ref[...] = (acc * scale).astype(jnp.bfloat16)
    best = jnp.max(top, axis=1, keepdims=True)
    eye = lax.broadcasted_iota(jnp.int32, (half, half), 0) == lax.broadcasted_iota(
        jnp.int32, (half, half), 1
    )
    lines = [
        jnp.max(jnp.where(eye, best[at : at + half], -1.0), axis=0, keepdims=True)
        for at in (0, half)
    ]
    out_top[...] = jnp.concatenate(lines, axis=0)


def after(x, *before):
    return lax.optimization_barrier((x, *before))[0]


def per_device(embeddings, dest_pos, cluster_lengths, block_mask):
    rows, width = embeddings.shape
    half = rows // 2
    count = lax.axis_size("blk")
    clusters = cluster_lengths.shape[0]
    steps = count // 4
    ahead, back = ring_perm(count, 1), ring_perm(count, -1)
    sibling = [(i, i ^ 1) for i in range(count)]

    def move(x, perm):
        return lax.ppermute(x, "blk", perm)

    def bf(n, w=width):
        return jax.ShapeDtypeStruct((n, w), jnp.bfloat16)

    def f32(*s):
        return jax.ShapeDtypeStruct(s, jnp.float32)

    full = half + TAIL
    wide = width + LANES
    state = f32(rows, wide)
    a, b, ah, bh = call(
        prep_body, [bf(full), bf(full), bf(half), bf(half)], [VM, VM],
    )(embeddings, dest_pos.reshape(2, half).astype(jnp.float32))

    lead = [(move(a, ahead), move(b, back))]
    follow = [(move(bh, ahead), move(ah, back))]
    sa, sb = move(a, sibling), move(b, sibling)
    work = 8 * rows * rows * width * WEIGHT
    own, sib, info, feat = call(
        functools.partial(first_body, half, clusters),
        [state, state, f32(2, 2 * rows, LANES), bf(2 * rows, count * clusters)],
        [SM, HB] + [VM] * 6, work,
        scratch=[pltpu.VMEM(block_mask.shape, jnp.int32), pltpu.SemaphoreType.DMA((1,))],
    )(cluster_lengths, block_mask, a, b, sa, sb, *lead[0])

    def middle(own, sib, keys, groups, work):
        return call(
            functools.partial(middle_body, half, clusters, groups), [state, state],
            [SM] + [VM] * (8 + len(keys)), work, aliases={7: 0, 8: 1},
        )(cluster_lengths, info, feat, a, b, sa, sb, own, sib, *keys)

    both = ((0, 0, 0), (1, 1, 1))
    for step in range(1, steps):
        f, g = lead[-1]
        lead.append((move(after(f, sa), ahead), move(after(g, sb), back)))
        if step > 1:
            own, sib = middle(
                own, sib, (*lead[-2], *follow[-2], *lead[-3]), (((2, 4, 1), (3, 5, 0)), both),
                work,
            )
        if step < steps - 1:
            f, g = follow[-1]
            follow.append((move(after(f, own), ahead), move(after(g, own), back)))
    own, sib = middle(own, sib, (*lead[-2], *follow[-1]), (((2, 0, 1), (3, 1, 0)),), 1)
    got = move(sib, sibling)
    far = [move(after(x, own), sibling) for x in lead[-1]]
    shared = (cluster_lengths, info, feat, a, b)
    own = call(
        functools.partial(late_body, half, clusters), [state], [SM] + [VM] * 7, work, aliases={5: 0},
    )(*shared, own, *lead[-1])[0]
    out_dir, out_top = call(
        functools.partial(last_body, half, clusters, (both,)),
        [bf(rows), f32(2, half)], [SM] + [VM] * 8,
    )(*shared, own, got, *far)
    return out_top.reshape(rows), out_dir


def solution(mesh):
    placed = (P(("groups", "blk"), None), P(("groups", "blk")), P("groups"), P("groups", None))
    return jax.shard_map(
        per_device,
        mesh=mesh,
        in_specs=placed,
        out_specs=(P(("groups", "blk")), P(("groups", "blk"), None)),
        check_vma=False,
    )
```

```python
import functools
import math

import jax
import jax.numpy as jnp
from jax import lax
from jax.experimental import pallas as pl
from jax.experimental.pallas import tpu as pltpu
from jax.sharding import PartitionSpec as P

EPS = 1e-06
TEMP = 4.0
LANES = 128
SPLIT = 128.0
TAIL = 8
VMEM_LIMIT = 16 * 1024 * 1024
PARTS = 2
WEIGHT = 20


def ring_order(chips):
    if chips <= 8:
        return list(range(0, chips, 2)) + list(range(1, chips, 2))[::-1]
    return list(range(chips))


def ring_perm(count, shift):
    order = ring_order(count // 2)
    pairs = []
    for at, chip in enumerate(order):
        to = order[(at + shift) % len(order)]
        pairs += [(2 * chip + core, 2 * to + core) for core in range(2)]
    return pairs


VM = pl.BlockSpec(memory_space=pltpu.VMEM)
SM = pl.BlockSpec(memory_space=pltpu.SMEM)
HB = pl.BlockSpec(memory_space=pltpu.HBM)


def call(body, out_shape, in_specs, flops=1, out_specs=None, scratch=(), aliases=None,
         limit=VMEM_LIMIT):
    return pl.pallas_call(
        body,
        out_shape=out_shape,
        in_specs=in_specs,
        out_specs=out_specs or [VM] * len(out_shape),
        scratch_shapes=list(scratch),
        input_output_aliases=aliases or {},
        compiler_params=pltpu.CompilerParams(vmem_limit_bytes=limit),
        cost_estimate=pl.CostEstimate(flops=flops, bytes_accessed=1, transcendentals=0),
    )


def prep_body(parts, emb_hbm, pos_hbm, a_ref, b_ref, ah_ref, bh_ref, emb_ref, pos_ref, sem):
    half = pos_ref.shape[1]
    rows, width = emb_ref.shape
    size = rows // parts
    fetch = []
    for i in range(parts):
        part = pl.ds(i * size, size)
        fetch.append(pltpu.make_async_copy(emb_hbm.at[part], emb_ref.at[part], sem.at[i]))
    last = pltpu.make_async_copy(pos_hbm, pos_ref, sem.at[parts])
    for copy in (*fetch, last):
        copy.start()
    for i, copy in enumerate(fetch):
        copy.wait()
        first = i * size
        whole, alone = (a_ref, ah_ref) if first < half else (b_ref, bh_ref)
        emb = emb_ref[first : first + size, :]
        unit = emb * lax.rsqrt(jnp.sum(emb * emb, axis=1, keepdims=True) + EPS)
        unit = unit.astype(jnp.bfloat16)
        for at in range(0, width, LANES):
            panel = unit[:, at : at + LANES]
            row = at // LANES * half + first % half
            alone[row : row + size] = panel
            whole[row : row + size] = panel
    last.wait()
    pos = pos_ref[...].astype(jnp.float32)
    high = jnp.floor(pos * (1.0 / SPLIT))
    low = pos - high * SPLIT
    tail = jnp.concatenate(
        [high[0:1], low[0:1], high[1:2], low[1:2], jnp.zeros((TAIL - 4, half), jnp.float32)],
        axis=0,
    ).astype(jnp.bfloat16)
    for ref in (a_ref, b_ref):
        ref[width // LANES * half :] = tail


def rows_of(ref, half):
    panels = ref.shape[0] // half
    return jnp.concatenate([ref[i * half : (i + 1) * half] for i in range(panels)], axis=1)


def positions_of(ref, half):
    tail = ref[ref.shape[0] // half * half :].astype(jnp.float32)
    return [tail[2 * i : 2 * i + 1] * SPLIT + tail[2 * i + 1 : 2 * i + 2] for i in range(2)]


def column(row):
    size = row.shape[1]
    eye = lax.broadcasted_iota(jnp.int32, (size, size), 0) == lax.broadcasted_iota(
        jnp.int32, (size, size), 1
    )
    return jnp.sum(jnp.where(eye, row, 0.0), axis=1, keepdims=True)


def cluster_parts(pos, ends, clusters):
    index = jnp.zeros(pos.shape, jnp.int32)
    start = jnp.zeros(pos.shape, jnp.float32)
    for c in range(clusters - 1):
        past = pos >= ends[c]
        index = index + past.astype(jnp.int32)
        start = jnp.where(past, ends[c], start)
    return index, start


def ends_of(len_ref, clusters):
    ends, total = [], jnp.int32(0)
    for c in range(clusters - 1):
        total = total + len_ref[c]
        ends.append(total.astype(jnp.float32))
    return ends


def attend(
    rows, query, pos_b, start_b, feat, acc, top, keys, key_pos, ends, clusters, diagonal
):
    index, _ = cluster_parts(key_pos, ends, clusters)
    block = jnp.floor(key_pos * (1.0 / rows)).astype(jnp.int32)
    wanted = block * clusters + index
    size = key_pos.shape[1]
    onehot = (
        lax.broadcasted_iota(jnp.int32, (feat.shape[1], size), 0) == wanted
    ).astype(jnp.bfloat16)
    allowed = jnp.dot(feat, onehot, preferred_element_type=jnp.float32)
    scores = lax.dot_general(
        query, keys, (((1,), (1,)), ((), ())), preferred_element_type=jnp.float32
    )
    weights = []
    for at in range(0, size, LANES):
        part = scores[:, at : at + LANES]
        pos = key_pos[:, at : at + LANES]
        earlier = (pos < pos_b) & (pos >= start_b)
        top = jnp.maximum(top, jnp.where(earlier, part, -1.0))
        weight = jnp.exp2(part * (TEMP * math.log2(math.e)))
        masked = weight * allowed[:, at : at + LANES]
        if diagonal:
            masked = jnp.where(pos == pos_b, weight, masked)
        weights.append(masked.astype(jnp.bfloat16))
    acc = acc + jnp.dot(
        jnp.concatenate(weights, axis=1), keys, preferred_element_type=jnp.float32
    )
    return acc, top


def column_parts(top):
    rest = jnp.max(top, axis=1, keepdims=True)
    lane = lax.broadcasted_iota(jnp.int32, top.shape, 1)
    out = jnp.zeros(top.shape, jnp.float32)
    for i in range(3):
        part = rest.astype(jnp.bfloat16).astype(jnp.float32)
        out = jnp.where(lane == i, part, out)
        rest = rest - part
    return out


def fold(rows, width, state, out_ref, query, info, feat, blocks, ends, clusters, diagonal=False):
    acc, top = state[:, :width], state[:, width:]
    for i, (keys, pos) in enumerate(blocks):
        acc, top = attend(
            rows, query, info[0], info[1], feat, acc, top, keys, pos, ends, clusters,
            diagonal and i == 0,
        )
    if out_ref.dtype == jnp.bfloat16:
        top = column_parts(top)
    out_ref[:, :width] = acc.astype(out_ref.dtype)
    out_ref[:, width:] = top.astype(out_ref.dtype)


def first_body(half, clusters, len_ref, mask_hbm, a_ref, b_ref, sa_ref, sb_ref,
               f_ref, g_ref, own_ref, sib_ref, info_ref, feat_ref, ends_ref, mask_ref, sem):
    fetch = pltpu.make_async_copy(mask_hbm, mask_ref, sem.at[0])
    fetch.start()
    ends = ends_of(len_ref, clusters)
    own = positions_of(a_ref, half)
    sib = positions_of(sa_ref, half)
    pos = jnp.concatenate([column(r) for r in own + sib], axis=0)
    index, start = cluster_parts(pos, ends, clusters)
    count = mask_ref.shape[0]
    rows = 2 * half
    width = a_ref.shape[0] // half * LANES
    block = jnp.floor(pos * (1.0 / rows)).astype(jnp.int32)
    total = pos.shape[0]
    onehot = (block == lax.broadcasted_iota(jnp.int32, (total, count), 1)).astype(jnp.bfloat16)
    wide = count * clusters
    spread = (
        lax.broadcasted_iota(jnp.int32, (count, wide), 1) // clusters
        == lax.broadcasted_iota(jnp.int32, (count, wide), 0)
    ).astype(jnp.bfloat16)
    fetch.wait()
    picked = jnp.dot(
        onehot, mask_ref[...].astype(jnp.bfloat16), preferred_element_type=jnp.float32
    ).astype(jnp.bfloat16)
    picked = jnp.dot(picked, spread, preferred_element_type=jnp.float32)
    lane_cluster = lax.broadcasted_iota(jnp.int32, (total, wide), 1) % clusters
    feat = jnp.where(lane_cluster == index, picked, 0.0).astype(jnp.bfloat16)
    feat_ref[...] = feat
    info_ref[0] = jnp.broadcast_to(pos, (total, LANES))
    info_ref[1] = jnp.broadcast_to(start, (total, LANES))
    keys = jnp.concatenate([rows_of(r, half) for r in (a_ref, b_ref)], axis=0)
    blocks = [(keys, jnp.concatenate(own, axis=1))]
    blocks += gather_keys((f_ref, g_ref), (((0, 0, 0), (1, 1, 1)),), half)
    state = jnp.concatenate(
        [jnp.zeros((rows, width), jnp.float32), jnp.full((rows, LANES), -1.0, jnp.float32)],
        axis=1,
    )
    ends_ref[...] = jnp.concatenate(
        [jnp.full((1, rows), e, jnp.float32) for e in ends]
        + [jnp.zeros((ends_ref.shape[0] - len(ends), rows), jnp.float32)],
        axis=0,
    )
    fold(rows, width, state, own_ref, keys, info_ref[:, :rows], feat[:rows], blocks, ends,
         clusters, True)
    other = jnp.concatenate([rows_of(r, half) for r in (sa_ref, sb_ref)], axis=0)
    fold(rows, width, state, sib_ref, other, info_ref[:, rows:], feat[rows:], blocks, ends,
         clusters)


def gather_keys(key_refs, groups, half):
    out = []
    for group in groups:
        keys = jnp.concatenate([rows_of(key_refs[r], half) for r, _, _ in group], axis=0)
        pos = jnp.concatenate(
            [positions_of(key_refs[p], half)[w] for _, p, w in group], axis=1
        )
        out.append((keys, pos))
    return out


def middle_body(half, clusters, groups, ends_ref, info_ref, feat_ref, a_ref, b_ref, sa_ref,
                sb_ref, own_in, sib_in, *refs):
    key_refs, (own_ref, sib_ref) = refs[:-2], refs[-2:]
    ends = [ends_ref[c : c + 1, :] for c in range(clusters - 1)]
    rows, width = 2 * half, a_ref.shape[0] // half * LANES
    blocks = gather_keys(key_refs, groups, half)
    for i, state_in, state_out, pair in (
        (0, own_in, own_ref, (a_ref, b_ref)), (1, sib_in, sib_ref, (sa_ref, sb_ref))
    ):
        query = jnp.concatenate([rows_of(r, half) for r in pair], axis=0)
        part = slice(i * rows, (i + 1) * rows)
        fold(rows, width, state_in[...], state_out, query, info_ref[:, part], feat_ref[part],
             blocks, ends, clusters)


def late_body(half, clusters, ends_ref, info_ref, feat_ref, a_ref, b_ref, own_in, *refs):
    key_refs, own_ref = refs[:-1], refs[-1]
    ends = [ends_ref[c : c + 1, :] for c in range(clusters - 1)]
    rows, width = 2 * half, a_ref.shape[0] // half * LANES
    blocks = gather_keys(key_refs, (((0, 0, 0), (1, 1, 1)),), half)
    query = jnp.concatenate([rows_of(r, half) for r in (a_ref, b_ref)], axis=0)
    fold(rows, width, own_in[...], own_ref, query, info_ref[:, :rows], feat_ref[:rows],
         blocks, ends, clusters)


def last_body(half, clusters, groups, ends_ref, info_ref, feat_ref, a_ref, b_ref, own_in, got_ref,
              *refs):
    key_refs, (dir_ref, out_top) = refs[:-2], refs[-2:]
    ends = [ends_ref[c : c + 1, :] for c in range(clusters - 1)]
    rows, width = 2 * half, a_ref.shape[0] // half * LANES
    query = jnp.concatenate([rows_of(r, half) for r in (a_ref, b_ref)], axis=0)
    acc = own_in[:, :width] + got_ref[:, :width].astype(jnp.float32)
    parts = got_ref[:, width:].astype(jnp.float32)
    top = jnp.maximum(own_in[:, width:], jnp.sum(parts, axis=1, keepdims=True))
    for keys, pos in gather_keys(key_refs, groups, half):
        acc, top = attend(
            rows, query, info_ref[0, :rows], info_ref[1, :rows], feat_ref[:rows], acc, top, keys,
            pos, ends, clusters, False,
        )
    scale = math.sqrt(width) * lax.rsqrt(jnp.sum(acc * acc, axis=1, keepdims=True) + EPS)
    dir_ref[...] = (acc * scale).astype(jnp.bfloat16)
    best = jnp.max(top, axis=1, keepdims=True)
    eye = lax.broadcasted_iota(jnp.int32, (half, half), 0) == lax.broadcasted_iota(
        jnp.int32, (half, half), 1
    )
    lines = [
        jnp.max(jnp.where(eye, best[at : at + half], -1.0), axis=0, keepdims=True)
        for at in (0, half)
    ]
    out_top[...] = jnp.concatenate(lines, axis=0)


def in_hbm(x):
    return pltpu.with_memory_space_constraint(x, pltpu.HBM)


def after(x, *before):
    return lax.optimization_barrier((x, *before))[0]


def per_device(embeddings, dest_pos, cluster_lengths, block_mask):
    rows, width = embeddings.shape
    half = rows // 2
    count = lax.axis_size("blk")
    clusters = cluster_lengths.shape[0]
    steps = count // 4
    ahead, back = ring_perm(count, 1), ring_perm(count, -1)
    sibling = [(i, i ^ 1) for i in range(count)]

    def move(x, perm):
        return lax.ppermute(x, "blk", perm)

    def bf(n, w=width):
        return jax.ShapeDtypeStruct((n, w), jnp.bfloat16)

    def f32(*s):
        return jax.ShapeDtypeStruct(s, jnp.float32)

    full = width // LANES * half + TAIL
    wide = width + LANES
    state = f32(rows, wide)
    a, b, ah, bh = call(
        functools.partial(prep_body, PARTS),
        [bf(full, LANES)] * 2 + [bf(full - TAIL, LANES)] * 2, [HB, HB],
        scratch=[
            pltpu.VMEM((rows, width), jnp.float32), pltpu.VMEM((2, half), jnp.int32),
            pltpu.SemaphoreType.DMA((PARTS + 1,)),
        ],
    )(in_hbm(embeddings), in_hbm(dest_pos.reshape(2, half)))

    lead = [(move(a, ahead), move(b, back))]
    follow = [(move(bh, ahead), move(ah, back))]
    sa, sb = move(a, sibling), move(b, sibling)
    work = 8 * rows * rows * width * WEIGHT
    own, sib, info, feat, ends = call(
        functools.partial(first_body, half, clusters),
        [state, state, f32(2, 2 * rows, LANES), bf(2 * rows, count * clusters),
         f32(-(-clusters // 8) * 8, rows)],
        [SM, HB] + [VM] * 6, work,
        scratch=[pltpu.VMEM(block_mask.shape, jnp.int32), pltpu.SemaphoreType.DMA((1,))],
    )(cluster_lengths, block_mask, a, b, sa, sb, *lead[0])

    def middle(own, sib, keys, groups, work, sent=state):
        return call(
            functools.partial(middle_body, half, clusters, groups), [state, sent],
            [VM] * (9 + len(keys)), work, aliases={7: 0, 8: 1} if sent is state else {7: 0},
        )(ends, info, feat, a, b, sa, sb, own, sib, *keys)

    both = ((0, 0, 0), (1, 1, 1))
    for step in range(1, steps):
        f, g = lead[-1]
        lead.append((move(f, ahead), move(g, back)))
        if step > 1:
            own, sib = middle(
                own, sib, (*lead[-2], *follow[-2], *lead[-3]), (((2, 4, 1), (3, 5, 0)), both),
                work,
            )
        if step < steps - 1:
            f, g = follow[-1]
            follow.append((move(after(f, own), ahead), move(after(g, own), back)))
    own, sib = middle(own, sib, (*lead[-2], *follow[-1]), (((2, 0, 1), (3, 1, 0)),), 1,
                      bf(rows, wide))
    got = move(sib, sibling)
    far = [move(after(x, own), sibling) for x in lead[-1]]
    shared = (ends, info, feat, a, b)
    own = call(
        functools.partial(late_body, half, clusters), [state], [VM] * 8, work, aliases={5: 0},
    )(*shared, own, *lead[-1])[0]
    out_dir, out_top = call(
        functools.partial(last_body, half, clusters, (both,)),
        [bf(rows), f32(2, half)], [VM] * 9,
    )(*shared, own, got, *far)
    return out_top.reshape(rows), out_dir


def solution(mesh):
    placed = (P(("groups", "blk"), None), P(("groups", "blk")), P("groups"), P("groups", None))
    return jax.shard_map(
        per_device,
        mesh=mesh,
        in_specs=placed,
        out_specs=(P(("groups", "blk")), P(("groups", "blk"), None)),
        check_vma=False,
    )
```

```python
import functools
import math

import jax
import jax.numpy as jnp
from jax import lax
from jax.experimental import pallas as pl
from jax.experimental.pallas import tpu as pltpu
from jax.sharding import PartitionSpec as P

EPS = 1e-06
TEMP = 4.0
LANES = 128
SPLIT = 128.0
TAIL = 16
VMEM_LIMIT = 16 * 1024 * 1024
PARTS = 2
WEIGHT = 20


def ring_order(chips):
    if chips <= 8:
        return list(range(0, chips, 2)) + list(range(1, chips, 2))[::-1]
    return list(range(chips))


def ring_perm(count, shift):
    order = ring_order(count // 2)
    pairs = []
    for at, chip in enumerate(order):
        to = order[(at + shift) % len(order)]
        pairs += [(2 * chip + core, 2 * to + core) for core in range(2)]
    return pairs


VM = pl.BlockSpec(memory_space=pltpu.VMEM)
SM = pl.BlockSpec(memory_space=pltpu.SMEM)
HB = pl.BlockSpec(memory_space=pltpu.HBM)


def call(body, out_shape, in_specs, flops=1, out_specs=None, scratch=(), aliases=None,
         limit=VMEM_LIMIT):
    return pl.pallas_call(
        body,
        out_shape=out_shape,
        in_specs=in_specs,
        out_specs=out_specs or [VM] * len(out_shape),
        scratch_shapes=list(scratch),
        input_output_aliases=aliases or {},
        compiler_params=pltpu.CompilerParams(vmem_limit_bytes=limit),
        cost_estimate=pl.CostEstimate(flops=flops, bytes_accessed=1, transcendentals=0),
    )


def prep_body(parts, emb_hbm, pos_hbm, a_ref, b_ref, ah_ref, bh_ref, emb_ref, pos_ref, sem):
    half = pos_ref.shape[1]
    rows, width = emb_ref.shape
    size = rows // parts
    fetch = []
    for i in range(parts):
        part = pl.ds(i * size, size)
        fetch.append(pltpu.make_async_copy(emb_hbm.at[part], emb_ref.at[part], sem.at[i]))
    last = pltpu.make_async_copy(pos_hbm, pos_ref, sem.at[parts])
    for copy in (*fetch, last):
        copy.start()
    for i, copy in enumerate(fetch):
        copy.wait()
        first = i * size
        whole, alone = (a_ref, ah_ref) if first < half else (b_ref, bh_ref)
        emb = emb_ref[first : first + size, :]
        unit = emb * lax.rsqrt(jnp.sum(emb * emb, axis=1, keepdims=True) + EPS)
        unit = unit.astype(jnp.bfloat16)
        for at in range(0, width, LANES):
            panel = unit[:, at : at + LANES]
            row = at // LANES * half + first % half
            alone[row : row + size] = panel
            whole[row : row + size] = panel
    last.wait()
    pos = pos_ref[...].astype(jnp.float32)
    high = jnp.floor(pos * (1.0 / SPLIT))
    low = pos - high * SPLIT
    tail = jnp.concatenate(
        [high[0:1], low[0:1], high[1:2], low[1:2], jnp.zeros((TAIL - 4, half), jnp.float32)],
        axis=0,
    ).astype(jnp.bfloat16)
    for ref in (a_ref, b_ref):
        ref[width // LANES * half :] = tail


def rows_of(ref, half):
    panels = ref.shape[0] // half
    return jnp.concatenate([ref[i * half : (i + 1) * half] for i in range(panels)], axis=1)


def positions_of(ref, half):
    tail = ref[ref.shape[0] // half * half :].astype(jnp.float32)
    return [tail[2 * i : 2 * i + 1] * SPLIT + tail[2 * i + 1 : 2 * i + 2] for i in range(2)]


def column(row):
    size = row.shape[1]
    eye = lax.broadcasted_iota(jnp.int32, (size, size), 0) == lax.broadcasted_iota(
        jnp.int32, (size, size), 1
    )
    return jnp.sum(jnp.where(eye, row, 0.0), axis=1, keepdims=True)


def cluster_parts(pos, ends, clusters):
    index = jnp.zeros(pos.shape, jnp.int32)
    start = jnp.zeros(pos.shape, jnp.float32)
    for c in range(clusters - 1):
        past = pos >= ends[c]
        index = index + past.astype(jnp.int32)
        start = jnp.where(past, ends[c], start)
    return index, start


def ends_of(len_ref, clusters):
    ends, total = [], jnp.int32(0)
    for c in range(clusters - 1):
        total = total + len_ref[c]
        ends.append(total.astype(jnp.float32))
    return ends


def attend(
    rows, query, pos_b, start_b, feat, acc, top, keys, key_pos, ends, clusters, diagonal
):
    index, _ = cluster_parts(key_pos, ends, clusters)
    block = jnp.floor(key_pos * (1.0 / rows)).astype(jnp.int32)
    wanted = block * clusters + index
    size = key_pos.shape[1]
    onehot = (
        lax.broadcasted_iota(jnp.int32, (feat.shape[1], size), 0) == wanted
    ).astype(jnp.bfloat16)
    allowed = jnp.dot(feat, onehot, preferred_element_type=jnp.float32)
    scores = lax.dot_general(
        query, keys, (((1,), (1,)), ((), ())), preferred_element_type=jnp.float32
    )
    weights = []
    for at in range(0, size, LANES):
        part = scores[:, at : at + LANES]
        pos = key_pos[:, at : at + LANES]
        earlier = (pos < pos_b) & (pos >= start_b)
        top = jnp.maximum(top, jnp.where(earlier, part, -1.0))
        weight = jnp.exp2(part * (TEMP * math.log2(math.e)))
        masked = weight * allowed[:, at : at + LANES]
        if diagonal:
            masked = jnp.where(pos == pos_b, weight, masked)
        weights.append(masked.astype(jnp.bfloat16))
    acc = acc + jnp.dot(
        jnp.concatenate(weights, axis=1), keys, preferred_element_type=jnp.float32
    )
    return acc, top


def column_parts(top):
    rest = jnp.max(top, axis=1, keepdims=True)
    lane = lax.broadcasted_iota(jnp.int32, top.shape, 1)
    out = jnp.zeros(top.shape, jnp.float32)
    for i in range(3):
        part = rest.astype(jnp.bfloat16).astype(jnp.float32)
        out = jnp.where(lane == i, part, out)
        rest = rest - part
    return out


def fold(rows, width, state, out_ref, query, info, feat, blocks, ends, clusters, diagonal=False):
    acc, top = state[:, :width], state[:, width:]
    for i, (keys, pos) in enumerate(blocks):
        acc, top = attend(
            rows, query, info[0], info[1], feat, acc, top, keys, pos, ends, clusters,
            diagonal and i == 0,
        )
    if out_ref.dtype == jnp.bfloat16:
        top = column_parts(top)
    out_ref[:, :width] = acc.astype(out_ref.dtype)
    out_ref[:, width:] = top.astype(out_ref.dtype)


def first_body(half, clusters, len_ref, mask_hbm, a_ref, b_ref, sa_ref, sb_ref,
               f_ref, g_ref, own_ref, sib_ref, info_ref, feat_ref, ends_ref, mask_ref, sem):
    fetch = pltpu.make_async_copy(mask_hbm, mask_ref, sem.at[0])
    fetch.start()
    ends = ends_of(len_ref, clusters)
    own = positions_of(a_ref, half)
    sib = positions_of(sa_ref, half)
    pos = jnp.concatenate([column(r) for r in own + sib], axis=0)
    index, start = cluster_parts(pos, ends, clusters)
    count = mask_ref.shape[0]
    rows = 2 * half
    width = a_ref.shape[0] // half * LANES
    block = jnp.floor(pos * (1.0 / rows)).astype(jnp.int32)
    total = pos.shape[0]
    onehot = (block == lax.broadcasted_iota(jnp.int32, (total, count), 1)).astype(jnp.bfloat16)
    wide = count * clusters
    spread = (
        lax.broadcasted_iota(jnp.int32, (count, wide), 1) // clusters
        == lax.broadcasted_iota(jnp.int32, (count, wide), 0)
    ).astype(jnp.bfloat16)
    fetch.wait()
    picked = jnp.dot(
        onehot, mask_ref[...].astype(jnp.bfloat16), preferred_element_type=jnp.float32
    ).astype(jnp.bfloat16)
    picked = jnp.dot(picked, spread, preferred_element_type=jnp.float32)
    lane_cluster = lax.broadcasted_iota(jnp.int32, (total, wide), 1) % clusters
    feat = jnp.where(lane_cluster == index, picked, 0.0).astype(jnp.bfloat16)
    feat_ref[...] = feat
    info_ref[0] = jnp.broadcast_to(pos, (total, LANES))
    info_ref[1] = jnp.broadcast_to(start, (total, LANES))
    keys = jnp.concatenate([rows_of(r, half) for r in (a_ref, b_ref)], axis=0)
    blocks = [(keys, jnp.concatenate(own, axis=1))]
    blocks += gather_keys((f_ref, g_ref), (((0, 0, 0), (1, 1, 1)),), half)
    state = jnp.concatenate(
        [jnp.zeros((rows, width), jnp.float32), jnp.full((rows, LANES), -1.0, jnp.float32)],
        axis=1,
    )
    ends_ref[...] = jnp.concatenate(
        [jnp.full((1, rows), e, jnp.float32) for e in ends]
        + [jnp.zeros((ends_ref.shape[0] - len(ends), rows), jnp.float32)],
        axis=0,
    )
    fold(rows, width, state, own_ref, keys, info_ref[:, :rows], feat[:rows], blocks, ends,
         clusters, True)
    other = jnp.concatenate([rows_of(r, half) for r in (sa_ref, sb_ref)], axis=0)
    fold(rows, width, state, sib_ref, other, info_ref[:, rows:], feat[rows:], blocks, ends,
         clusters)


def gather_keys(key_refs, groups, half):
    out = []
    for group in groups:
        keys = jnp.concatenate([rows_of(key_refs[r], half) for r, _, _ in group], axis=0)
        pos = jnp.concatenate(
            [positions_of(key_refs[p], half)[w] for _, p, w in group], axis=1
        )
        out.append((keys, pos))
    return out


def middle_body(half, clusters, groups, ends_ref, info_ref, feat_ref, a_ref, b_ref, sa_ref,
                sb_ref, own_in, sib_in, *refs):
    key_refs, (own_ref, sib_ref) = refs[:-2], refs[-2:]
    ends = [ends_ref[c : c + 1, :] for c in range(clusters - 1)]
    rows, width = 2 * half, a_ref.shape[0] // half * LANES
    blocks = gather_keys(key_refs, groups, half)
    for i, state_in, state_out, pair in (
        (0, own_in, own_ref, (a_ref, b_ref)), (1, sib_in, sib_ref, (sa_ref, sb_ref))
    ):
        query = jnp.concatenate([rows_of(r, half) for r in pair], axis=0)
        part = slice(i * rows, (i + 1) * rows)
        fold(rows, width, state_in[...], state_out, query, info_ref[:, part], feat_ref[part],
             blocks, ends, clusters)


def late_body(half, clusters, ends_ref, info_ref, feat_ref, a_ref, b_ref, own_in, *refs):
    key_refs, own_ref = refs[:-1], refs[-1]
    ends = [ends_ref[c : c + 1, :] for c in range(clusters - 1)]
    rows, width = 2 * half, a_ref.shape[0] // half * LANES
    blocks = gather_keys(key_refs, (((0, 0, 0), (1, 1, 1)),), half)
    query = jnp.concatenate([rows_of(r, half) for r in (a_ref, b_ref)], axis=0)
    fold(rows, width, own_in[...], own_ref, query, info_ref[:, :rows], feat_ref[:rows],
         blocks, ends, clusters)


def join_body(state_ref, f_ref, out_ref):
    rows, wide = state_ref.shape
    panels = wide // LANES
    for i in range(panels):
        out_ref[i * rows : (i + 1) * rows] = state_ref[:, i * LANES : (i + 1) * LANES]
    out_ref[panels * rows : panels * rows + f_ref.shape[0]] = f_ref[...]


def last_body(half, clusters, ends_ref, info_ref, feat_ref, a_ref, b_ref, own_in, got_ref,
              far_ref, dir_ref, out_top):
    ends = [ends_ref[c : c + 1, :] for c in range(clusters - 1)]
    rows, width = 2 * half, a_ref.shape[0] // half * LANES
    query = jnp.concatenate([rows_of(r, half) for r in (a_ref, b_ref)], axis=0)
    panels = width // LANES
    parts = [got_ref[i * rows : (i + 1) * rows].astype(jnp.float32) for i in range(panels + 1)]
    acc = own_in[:, :width] + jnp.concatenate(parts[:panels], axis=1)
    top = jnp.maximum(own_in[:, width:], jnp.sum(parts[panels], axis=1, keepdims=True))
    key_refs = [got_ref.at[pl.ds((panels + 1) * rows, a_ref.shape[0])], far_ref]
    for keys, pos in gather_keys(key_refs, (((0, 0, 0), (1, 1, 1)),), half):
        acc, top = attend(
            rows, query, info_ref[0, :rows], info_ref[1, :rows], feat_ref[:rows], acc, top, keys,
            pos, ends, clusters, False,
        )
    scale = math.sqrt(width) * lax.rsqrt(jnp.sum(acc * acc, axis=1, keepdims=True) + EPS)
    dir_ref[...] = (acc * scale).astype(jnp.bfloat16)
    best = jnp.max(top, axis=1, keepdims=True)
    eye = lax.broadcasted_iota(jnp.int32, (half, half), 0) == lax.broadcasted_iota(
        jnp.int32, (half, half), 1
    )
    lines = [
        jnp.max(jnp.where(eye, best[at : at + half], -1.0), axis=0, keepdims=True)
        for at in (0, half)
    ]
    out_top[...] = jnp.concatenate(lines, axis=0)


def in_hbm(x):
    return pltpu.with_memory_space_constraint(x, pltpu.HBM)


def after(x, *before):
    return lax.optimization_barrier((x, *before))[0]


def per_device(embeddings, dest_pos, cluster_lengths, block_mask):
    rows, width = embeddings.shape
    half = rows // 2
    count = lax.axis_size("blk")
    clusters = cluster_lengths.shape[0]
    steps = count // 4
    ahead, back = ring_perm(count, -1), ring_perm(count, 1)
    sibling = [(i, i ^ 1) for i in range(count)]

    def move(x, perm):
        return lax.ppermute(x, "blk", perm)

    def bf(n, w=width):
        return jax.ShapeDtypeStruct((n, w), jnp.bfloat16)

    def f32(*s):
        return jax.ShapeDtypeStruct(s, jnp.float32)

    full = width // LANES * half + TAIL
    wide = width + LANES
    state = f32(rows, wide)
    a, b, ah, bh = call(
        functools.partial(prep_body, PARTS),
        [bf(full, LANES)] * 2 + [bf(full - TAIL, LANES)] * 2, [HB, HB],
        scratch=[
            pltpu.VMEM((rows, width), jnp.float32), pltpu.VMEM((2, half), jnp.int32),
            pltpu.SemaphoreType.DMA((PARTS + 1,)),
        ],
    )(in_hbm(embeddings), in_hbm(dest_pos.reshape(2, half)))

    lead = [(move(a, ahead), move(b, back))]
    follow = [(move(bh, ahead), move(ah, back))]
    sa, sb = move(a, sibling), move(b, sibling)
    work = 8 * rows * rows * width * WEIGHT
    own, sib, info, feat, ends = call(
        functools.partial(first_body, half, clusters),
        [state, state, f32(2, 2 * rows, LANES), bf(2 * rows, count * clusters),
         f32(-(-clusters // 8) * 8, rows)],
        [SM, HB] + [VM] * 6, work,
        scratch=[pltpu.VMEM(block_mask.shape, jnp.int32), pltpu.SemaphoreType.DMA((1,))],
    )(cluster_lengths, block_mask, a, b, sa, sb, *lead[0])

    def middle(own, sib, keys, groups, work, sent=state):
        return call(
            functools.partial(middle_body, half, clusters, groups), [state, sent],
            [VM] * (9 + len(keys)), work, aliases={7: 0, 8: 1} if sent is state else {7: 0},
        )(ends, info, feat, a, b, sa, sb, own, sib, *keys)

    both = ((0, 0, 0), (1, 1, 1))
    for step in range(1, steps):
        f, g = lead[-1]
        lead.append((move(f, ahead), move(g, back)))
        if step > 1:
            own, sib = middle(
                own, sib, (*lead[-2], *follow[-2], *lead[-3]), (((2, 4, 1), (3, 5, 0)), both),
                work,
            )
        if step < steps - 1:
            f, g = follow[-1]
            follow.append((move(after(f, own), ahead), move(after(g, own), back)))
    own, sib = middle(own, sib, (*lead[-2], *follow[-1]), (((2, 0, 1), (3, 1, 0)),), 1,
                      bf(rows, wide))
    stacked = wide // LANES * rows + -(-full // 16) * 16
    joined = call(join_body, [bf(stacked, LANES)], [VM, VM])(sib, lead[-1][0])[0]
    got = move(joined, sibling)
    far = move(after(lead[-1][1], own), sibling)
    shared = (ends, info, feat, a, b)
    own = call(
        functools.partial(late_body, half, clusters), [state], [VM] * 8, work, aliases={5: 0},
    )(*shared, own, *lead[-1])[0]
    out_dir, out_top = call(
        functools.partial(last_body, half, clusters),
        [bf(rows), f32(2, half)], [VM] * 8,
    )(*shared, own, got, far)
    return out_top.reshape(rows), out_dir


def solution(mesh):
    placed = (P(("groups", "blk"), None), P(("groups", "blk")), P("groups"), P("groups", None))
    return jax.shard_map(
        per_device,
        mesh=mesh,
        in_specs=placed,
        out_specs=(P(("groups", "blk")), P(("groups", "blk"), None)),
        check_vma=False,
    )
```

```python
import functools
import math

import jax
import jax.numpy as jnp
from jax import lax
from jax.experimental import pallas as pl
from jax.experimental.pallas import tpu as pltpu
from jax.sharding import PartitionSpec as P

EPS = 1e-06
TEMP = 4.0
LANES = 128
SPLIT = 128.0
TAIL = 16
VMEM_LIMIT = 16 * 1024 * 1024
PARTS = 2
WEIGHT = 20


def ring_order(chips):
    if chips <= 8:
        return list(range(0, chips, 2)) + list(range(1, chips, 2))[::-1]
    return list(range(chips))


def ring_perm(count, shift):
    order = ring_order(count // 2)
    pairs = []
    for at, chip in enumerate(order):
        to = order[(at + shift) % len(order)]
        pairs += [(2 * chip + core, 2 * to + core) for core in range(2)]
    return pairs


VM = pl.BlockSpec(memory_space=pltpu.VMEM)
SM = pl.BlockSpec(memory_space=pltpu.SMEM)
HB = pl.BlockSpec(memory_space=pltpu.HBM)


def call(body, out_shape, in_specs, flops=1, out_specs=None, scratch=(), aliases=None,
         limit=VMEM_LIMIT):
    return pl.pallas_call(
        body,
        out_shape=out_shape,
        in_specs=in_specs,
        out_specs=out_specs or [VM] * len(out_shape),
        scratch_shapes=list(scratch),
        input_output_aliases=aliases or {},
        compiler_params=pltpu.CompilerParams(vmem_limit_bytes=limit),
        cost_estimate=pl.CostEstimate(flops=flops, bytes_accessed=1, transcendentals=0),
    )


def prep_body(parts, emb_hbm, pos_hbm, a_ref, b_ref, ah_ref, bh_ref, emb_ref, pos_ref, sem):
    half = pos_ref.shape[1]
    rows, width = emb_ref.shape
    size = rows // parts
    fetch = []
    for i in range(parts):
        part = pl.ds(i * size, size)
        fetch.append(pltpu.make_async_copy(emb_hbm.at[part], emb_ref.at[part], sem.at[i]))
    last = pltpu.make_async_copy(pos_hbm, pos_ref, sem.at[parts])
    for copy in (*fetch, last):
        copy.start()
    for i, copy in enumerate(fetch):
        copy.wait()
        first = i * size
        whole, alone = (a_ref, ah_ref) if first < half else (b_ref, bh_ref)
        emb = emb_ref[first : first + size, :]
        unit = emb * lax.rsqrt(jnp.sum(emb * emb, axis=1, keepdims=True) + EPS)
        unit = unit.astype(jnp.bfloat16)
        for at in range(0, width, LANES):
            panel = unit[:, at : at + LANES]
            row = at // LANES * half + first % half
            alone[row : row + size] = panel
            whole[row : row + size] = panel
    last.wait()
    pos = pos_ref[...].astype(jnp.float32)
    high = jnp.floor(pos * (1.0 / SPLIT))
    low = pos - high * SPLIT
    tail = jnp.concatenate(
        [high[0:1], low[0:1], high[1:2], low[1:2], jnp.zeros((TAIL - 4, half), jnp.float32)],
        axis=0,
    ).astype(jnp.bfloat16)
    for ref in (a_ref, b_ref):
        ref[width // LANES * half :] = tail


def rows_of(ref, half):
    panels = ref.shape[0] // half
    return jnp.concatenate([ref[i * half : (i + 1) * half] for i in range(panels)], axis=1)


def positions_of(ref, half):
    tail = ref[ref.shape[0] // half * half :].astype(jnp.float32)
    return [tail[2 * i : 2 * i + 1] * SPLIT + tail[2 * i + 1 : 2 * i + 2] for i in range(2)]


def column(row):
    size = row.shape[1]
    eye = lax.broadcasted_iota(jnp.int32, (size, size), 0) == lax.broadcasted_iota(
        jnp.int32, (size, size), 1
    )
    return jnp.sum(jnp.where(eye, row, 0.0), axis=1, keepdims=True)


def cluster_parts(pos, ends, clusters):
    index = jnp.zeros(pos.shape, jnp.int32)
    start = jnp.zeros(pos.shape, jnp.float32)
    for c in range(clusters - 1):
        past = pos >= ends[c]
        index = index + past.astype(jnp.int32)
        start = jnp.where(past, ends[c], start)
    return index, start


def ends_of(len_ref, clusters):
    ends, total = [], jnp.int32(0)
    for c in range(clusters - 1):
        total = total + len_ref[c]
        ends.append(total.astype(jnp.float32))
    return ends


def attend(
    rows, query, pos_b, start_b, feat, acc, top, keys, key_pos, ends, clusters, diagonal
):
    index, _ = cluster_parts(key_pos, ends, clusters)
    block = jnp.floor(key_pos * (1.0 / rows)).astype(jnp.int32)
    wanted = block * clusters + index
    size = key_pos.shape[1]
    onehot = (
        lax.broadcasted_iota(jnp.int32, (feat.shape[1], size), 0) == wanted
    ).astype(jnp.bfloat16)
    allowed = jnp.dot(feat, onehot, preferred_element_type=jnp.float32)
    scores = lax.dot_general(
        query, keys, (((1,), (1,)), ((), ())), preferred_element_type=jnp.float32
    )
    weights = []
    for at in range(0, size, LANES):
        part = scores[:, at : at + LANES]
        pos = key_pos[:, at : at + LANES]
        earlier = (pos < pos_b) & (pos >= start_b)
        top = jnp.maximum(top, jnp.where(earlier, part, -1.0))
        weight = jnp.exp2(part * (TEMP * math.log2(math.e)))
        masked = weight * allowed[:, at : at + LANES]
        if diagonal:
            masked = jnp.where(pos == pos_b, weight, masked)
        weights.append(masked.astype(jnp.bfloat16))
    acc = acc + jnp.dot(
        jnp.concatenate(weights, axis=1), keys, preferred_element_type=jnp.float32
    )
    return acc, top


def column_parts(top):
    rest = jnp.max(top, axis=1, keepdims=True)
    lane = lax.broadcasted_iota(jnp.int32, top.shape, 1)
    out = jnp.zeros(top.shape, jnp.float32)
    for i in range(3):
        part = rest.astype(jnp.bfloat16).astype(jnp.float32)
        out = jnp.where(lane == i, part, out)
        rest = rest - part
    return out


def fold(rows, width, state, out_ref, query, info, feat, blocks, ends, clusters, diagonal=False):
    acc, top = state[:, :width], state[:, width:]
    for i, (keys, pos) in enumerate(blocks):
        acc, top = attend(
            rows, query, info[0], info[1], feat, acc, top, keys, pos, ends, clusters,
            diagonal and i == 0,
        )
    if out_ref.dtype == jnp.bfloat16:
        top = column_parts(top)
    out_ref[:, :width] = acc.astype(out_ref.dtype)
    out_ref[:, width:] = top.astype(out_ref.dtype)


def first_body(half, clusters, len_ref, mask_hbm, a_ref, b_ref, sa_ref, sb_ref,
               f_ref, g_ref, own_ref, sib_ref, info_ref, feat_ref, ends_ref, mask_ref, sem):
    fetch = pltpu.make_async_copy(mask_hbm, mask_ref, sem.at[0])
    fetch.start()
    ends = ends_of(len_ref, clusters)
    own = positions_of(a_ref, half)
    sib = positions_of(sa_ref, half)
    pos = jnp.concatenate([column(r) for r in own + sib], axis=0)
    index, start = cluster_parts(pos, ends, clusters)
    count = mask_ref.shape[0]
    rows = 2 * half
    width = a_ref.shape[0] // half * LANES
    block = jnp.floor(pos * (1.0 / rows)).astype(jnp.int32)
    total = pos.shape[0]
    onehot = (block == lax.broadcasted_iota(jnp.int32, (total, count), 1)).astype(jnp.bfloat16)
    wide = count * clusters
    spread = (
        lax.broadcasted_iota(jnp.int32, (count, wide), 1) // clusters
        == lax.broadcasted_iota(jnp.int32, (count, wide), 0)
    ).astype(jnp.bfloat16)
    fetch.wait()
    picked = jnp.dot(
        onehot, mask_ref[...].astype(jnp.bfloat16), preferred_element_type=jnp.float32
    ).astype(jnp.bfloat16)
    picked = jnp.dot(picked, spread, preferred_element_type=jnp.float32)
    lane_cluster = lax.broadcasted_iota(jnp.int32, (total, wide), 1) % clusters
    feat = jnp.where(lane_cluster == index, picked, 0.0).astype(jnp.bfloat16)
    feat_ref[...] = feat
    info_ref[0] = jnp.broadcast_to(pos, (total, LANES))
    info_ref[1] = jnp.broadcast_to(start, (total, LANES))
    keys = jnp.concatenate([rows_of(r, half) for r in (a_ref, b_ref)], axis=0)
    blocks = [(keys, jnp.concatenate(own, axis=1))]
    blocks += gather_keys((f_ref, g_ref), (((0, 0, 0), (1, 1, 1)),), half)
    state = jnp.concatenate(
        [jnp.zeros((rows, width), jnp.float32), jnp.full((rows, LANES), -1.0, jnp.float32)],
        axis=1,
    )
    ends_ref[...] = jnp.concatenate(
        [jnp.full((1, rows), e, jnp.float32) for e in ends]
        + [jnp.zeros((ends_ref.shape[0] - len(ends), rows), jnp.float32)],
        axis=0,
    )
    fold(rows, width, state, own_ref, keys, info_ref[:, :rows], feat[:rows], blocks, ends,
         clusters, True)
    other = jnp.concatenate([rows_of(r, half) for r in (sa_ref, sb_ref)], axis=0)
    fold(rows, width, state, sib_ref, other, info_ref[:, rows:], feat[rows:], blocks, ends,
         clusters)


def gather_keys(key_refs, groups, half):
    out = []
    for group in groups:
        keys = jnp.concatenate([rows_of(key_refs[r], half) for r, _, _ in group], axis=0)
        pos = jnp.concatenate(
            [positions_of(key_refs[p], half)[w] for _, p, w in group], axis=1
        )
        out.append((keys, pos))
    return out


def middle_body(half, clusters, groups, ends_ref, info_ref, feat_ref, a_ref, b_ref, sa_ref,
                sb_ref, own_in, sib_in, *refs):
    key_refs, (own_ref, sib_ref) = refs[:-2], refs[-2:]
    ends = [ends_ref[c : c + 1, :] for c in range(clusters - 1)]
    rows, width = 2 * half, a_ref.shape[0] // half * LANES
    blocks = gather_keys(key_refs, groups, half)
    for i, state_in, state_out, pair in (
        (0, own_in, own_ref, (a_ref, b_ref)), (1, sib_in, sib_ref, (sa_ref, sb_ref))
    ):
        query = jnp.concatenate([rows_of(r, half) for r in pair], axis=0)
        part = slice(i * rows, (i + 1) * rows)
        fold(rows, width, state_in[...], state_out, query, info_ref[:, part], feat_ref[part],
             blocks, ends, clusters)


def late_body(half, clusters, ends_ref, info_ref, feat_ref, a_ref, b_ref, own_in, *refs):
    key_refs, own_ref = refs[:-1], refs[-1]
    ends = [ends_ref[c : c + 1, :] for c in range(clusters - 1)]
    rows, width = 2 * half, a_ref.shape[0] // half * LANES
    blocks = gather_keys(key_refs, (((0, 0, 0), (1, 1, 1)),), half)
    query = jnp.concatenate([rows_of(r, half) for r in (a_ref, b_ref)], axis=0)
    fold(rows, width, own_in[...], own_ref, query, info_ref[:, :rows], feat_ref[:rows],
         blocks, ends, clusters)


def join_body(state_ref, f_ref, out_ref):
    rows, wide = state_ref.shape
    panels = wide // LANES
    for i in range(panels):
        out_ref[i * rows : (i + 1) * rows] = state_ref[:, i * LANES : (i + 1) * LANES]
    out_ref[panels * rows : panels * rows + f_ref.shape[0]] = f_ref[...]


def last_body(half, clusters, ends_ref, info_ref, feat_ref, a_ref, b_ref, own_in, got_ref,
              far_ref, dir_hbm, top_hbm, dir_ref, top_ref, sem):
    ends = [ends_ref[c : c + 1, :] for c in range(clusters - 1)]
    rows, width = 2 * half, a_ref.shape[0] // half * LANES
    query = jnp.concatenate([rows_of(r, half) for r in (a_ref, b_ref)], axis=0)
    panels = width // LANES
    parts = [got_ref[i * rows : (i + 1) * rows].astype(jnp.float32) for i in range(panels + 1)]
    acc = own_in[:, :width] + jnp.concatenate(parts[:panels], axis=1)
    top = jnp.maximum(own_in[:, width:], jnp.sum(parts[panels], axis=1, keepdims=True))
    key_refs = [got_ref.at[pl.ds((panels + 1) * rows, a_ref.shape[0])], far_ref]
    for keys, pos in gather_keys(key_refs, (((0, 0, 0), (1, 1, 1)),), half):
        acc, top = attend(
            rows, query, info_ref[0, :rows], info_ref[1, :rows], feat_ref[:rows], acc, top, keys,
            pos, ends, clusters, False,
        )
    best = jnp.max(top, axis=1, keepdims=True)
    eye = lax.broadcasted_iota(jnp.int32, (half, half), 0) == lax.broadcasted_iota(
        jnp.int32, (half, half), 1
    )
    lines = [
        jnp.max(jnp.where(eye, best[at : at + half], -1.0), axis=0, keepdims=True)
        for at in (0, half)
    ]
    top_ref[...] = jnp.concatenate(lines, axis=0)
    sends = [pltpu.make_async_copy(top_ref, top_hbm, sem.at[2])]
    sends[0].start()
    for i in range(2):
        part = acc[i * half : (i + 1) * half]
        scale = math.sqrt(width) * lax.rsqrt(jnp.sum(part * part, axis=1, keepdims=True) + EPS)
        dir_ref[i * half : (i + 1) * half] = (part * scale).astype(jnp.bfloat16)
        place = pl.ds(i * half, half)
        sends.append(pltpu.make_async_copy(dir_ref.at[place], dir_hbm.at[place], sem.at[i]))
        sends[-1].start()
    for copy in sends:
        copy.wait()


def in_hbm(x):
    return pltpu.with_memory_space_constraint(x, pltpu.HBM)


def after(x, *before):
    return lax.optimization_barrier((x, *before))[0]


def per_device(embeddings, dest_pos, cluster_lengths, block_mask):
    rows, width = embeddings.shape
    half = rows // 2
    count = lax.axis_size("blk")
    clusters = cluster_lengths.shape[0]
    steps = count // 4
    ahead, back = ring_perm(count, -1), ring_perm(count, 1)
    sibling = [(i, i ^ 1) for i in range(count)]

    def move(x, perm):
        return lax.ppermute(x, "blk", perm)

    def bf(n, w=width):
        return jax.ShapeDtypeStruct((n, w), jnp.bfloat16)

    def f32(*s):
        return jax.ShapeDtypeStruct(s, jnp.float32)

    full = width // LANES * half + TAIL
    wide = width + LANES
    state = f32(rows, wide)
    a, b, ah, bh = call(
        functools.partial(prep_body, PARTS),
        [bf(full, LANES)] * 2 + [bf(full - TAIL, LANES)] * 2, [HB, HB],
        scratch=[
            pltpu.VMEM((rows, width), jnp.float32), pltpu.VMEM((2, half), jnp.int32),
            pltpu.SemaphoreType.DMA((PARTS + 1,)),
        ],
    )(in_hbm(embeddings), in_hbm(dest_pos.reshape(2, half)))

    lead = [(move(a, ahead), move(b, back))]
    follow = [(move(bh, ahead), move(ah, back))]
    sa, sb = move(a, sibling), move(b, sibling)
    work = 8 * rows * rows * width * WEIGHT
    own, sib, info, feat, ends = call(
        functools.partial(first_body, half, clusters),
        [state, state, f32(2, 2 * rows, LANES), bf(2 * rows, count * clusters),
         f32(-(-clusters // 8) * 8, rows)],
        [SM, HB] + [VM] * 6, work,
        scratch=[pltpu.VMEM(block_mask.shape, jnp.int32), pltpu.SemaphoreType.DMA((1,))],
    )(cluster_lengths, block_mask, a, b, sa, sb, *lead[0])

    def middle(own, sib, keys, groups, work, sent=state):
        return call(
            functools.partial(middle_body, half, clusters, groups), [state, sent],
            [VM] * (9 + len(keys)), work, aliases={7: 0, 8: 1} if sent is state else {7: 0},
        )(ends, info, feat, a, b, sa, sb, own, sib, *keys)

    both = ((0, 0, 0), (1, 1, 1))
    for step in range(1, steps):
        f, g = lead[-1]
        lead.append((move(f, ahead), move(g, back)))
        if step > 1:
            own, sib = middle(
                own, sib, (*lead[-2], *follow[-2], *lead[-3]), (((2, 4, 1), (3, 5, 0)), both),
                work,
            )
        if step < steps - 1:
            f, g = follow[-1]
            follow.append((move(after(f, own), ahead), move(after(g, own), back)))
    own, sib = middle(own, sib, (*lead[-2], *follow[-1]), (((2, 0, 1), (3, 1, 0)),), 1,
                      bf(rows, wide))
    stacked = wide // LANES * rows + -(-full // 16) * 16
    joined = call(join_body, [bf(stacked, LANES)], [VM, VM])(sib, lead[-1][0])[0]
    got = move(joined, sibling)
    far = move(after(lead[-1][1], own), sibling)
    shared = (ends, info, feat, a, b)
    own = call(
        functools.partial(late_body, half, clusters), [state], [VM] * 8, work, aliases={5: 0},
    )(*shared, own, *lead[-1])[0]
    out_dir, out_top = call(
        functools.partial(last_body, half, clusters),
        [bf(rows), f32(2, half)], [VM] * 8, out_specs=[HB, HB],
        scratch=[
            pltpu.VMEM((rows, width), jnp.bfloat16), pltpu.VMEM((2, half), jnp.float32),
            pltpu.SemaphoreType.DMA((3,)),
        ],
    )(*shared, own, got, far)
    return out_top.reshape(rows), out_dir


def solution(mesh):
    placed = (P(("groups", "blk"), None), P(("groups", "blk")), P("groups"), P("groups", None))
    return jax.shard_map(
        per_device,
        mesh=mesh,
        in_specs=placed,
        out_specs=(P(("groups", "blk")), P(("groups", "blk"), None)),
        check_vma=False,
    )
```

```python
import functools
import math

import jax
import jax.numpy as jnp
from jax import lax
from jax.experimental import pallas as pl
from jax.experimental.pallas import tpu as pltpu
from jax.sharding import PartitionSpec as P

EPS = 1e-06
TEMP = 4.0
LANES = 128
SPLIT = 128.0
TAIL = 16
VMEM_LIMIT = 16 * 1024 * 1024
WEIGHT = 20


def ring_order(chips):
    if chips <= 8:
        return list(range(0, chips, 2)) + list(range(1, chips, 2))[::-1]
    return list(range(chips))


def ring_perm(count, shift):
    order = ring_order(count // 2)
    pairs = []
    for at, chip in enumerate(order):
        to = order[(at + shift) % len(order)]
        pairs += [(2 * chip + core, 2 * to + core) for core in range(2)]
    return pairs


VM = pl.BlockSpec(memory_space=pltpu.VMEM)
SM = pl.BlockSpec(memory_space=pltpu.SMEM)
HB = pl.BlockSpec(memory_space=pltpu.HBM)


def call(body, out_shape, in_specs, flops=1, out_specs=None, scratch=(), aliases=None,
         limit=VMEM_LIMIT):
    return pl.pallas_call(
        body,
        out_shape=out_shape,
        in_specs=in_specs,
        out_specs=out_specs or [VM] * len(out_shape),
        scratch_shapes=list(scratch),
        input_output_aliases=aliases or {},
        compiler_params=pltpu.CompilerParams(vmem_limit_bytes=limit),
        cost_estimate=pl.CostEstimate(flops=flops, bytes_accessed=1, transcendentals=0),
    )


def prep_body(sizes, emb_hbm, pos_hbm, a_ref, b_ref, ah_ref, bh_ref, emb_ref, pos_ref, sem):
    width = emb_ref.shape[1]
    starts = (0, sizes[0])
    fetch = []
    for i, (first, size) in enumerate(zip(starts, sizes)):
        part = pl.ds(first, size)
        fetch.append(pltpu.make_async_copy(emb_hbm.at[part], emb_ref.at[part], sem.at[i]))
    last = pltpu.make_async_copy(pos_hbm, pos_ref, sem.at[2])
    for copy in (*fetch, last):
        copy.start()
    for i, copy in enumerate(fetch):
        copy.wait()
        first, size = starts[i], sizes[i]
        whole, alone = (a_ref, ah_ref) if i == 0 else (b_ref, bh_ref)
        emb = emb_ref[first : first + size, :]
        unit = emb * lax.rsqrt(jnp.sum(emb * emb, axis=1, keepdims=True) + EPS)
        unit = unit.astype(jnp.bfloat16)
        for at in range(0, width, LANES):
            panel = unit[:, at : at + LANES]
            row = at // LANES * size
            alone[row : row + size] = panel
            whole[row : row + size] = panel
    last.wait()
    pos = pos_ref[...].astype(jnp.float32)
    high = jnp.floor(pos * (1.0 / SPLIT))
    low = pos - high * SPLIT
    tail = jnp.concatenate(
        [high[0:1], low[0:1], high[1:2], low[1:2], jnp.zeros((TAIL - 4, LANES), jnp.float32)],
        axis=0,
    ).astype(jnp.bfloat16)
    for ref in (a_ref, b_ref):
        ref[ref.shape[0] - TAIL :] = tail


def rows_of(ref, width):
    panels = width // LANES
    size = ref.shape[0] // panels // 16 * 16
    return jnp.concatenate([ref[i * size : (i + 1) * size] for i in range(panels)], axis=1)


def positions_of(ref):
    tail = ref[ref.shape[0] - TAIL :].astype(jnp.float32)
    return [tail[2 * i : 2 * i + 1] * SPLIT + tail[2 * i + 1 : 2 * i + 2] for i in range(2)]


def column(row):
    size = row.shape[1]
    eye = lax.broadcasted_iota(jnp.int32, (size, size), 0) == lax.broadcasted_iota(
        jnp.int32, (size, size), 1
    )
    return jnp.sum(jnp.where(eye, row, 0.0), axis=1, keepdims=True)


def cluster_parts(pos, ends, clusters):
    index = jnp.zeros(pos.shape, jnp.int32)
    start = jnp.zeros(pos.shape, jnp.float32)
    for c in range(clusters - 1):
        past = pos >= ends[c]
        index = index + past.astype(jnp.int32)
        start = jnp.where(past, ends[c], start)
    return index, start


def ends_of(len_ref, clusters):
    ends, total = [], jnp.int32(0)
    for c in range(clusters - 1):
        total = total + len_ref[c]
        ends.append(total.astype(jnp.float32))
    return ends


def attend(
    rows, query, pos_b, start_b, feat, acc, top, keys, key_pos, ends, clusters, diagonal
):
    index, _ = cluster_parts(key_pos, ends, clusters)
    block = jnp.floor(key_pos * (1.0 / rows)).astype(jnp.int32)
    wanted = block * clusters + index
    size = key_pos.shape[1]
    onehot = (
        lax.broadcasted_iota(jnp.int32, (feat.shape[1], size), 0) == wanted
    ).astype(jnp.bfloat16)
    allowed = jnp.dot(feat, onehot, preferred_element_type=jnp.float32)
    scores = lax.dot_general(
        query, keys, (((1,), (1,)), ((), ())), preferred_element_type=jnp.float32
    )
    weights = []
    for at in range(0, size, LANES):
        part = scores[:, at : at + LANES]
        pos = key_pos[:, at : at + LANES]
        earlier = (pos < pos_b) & (pos >= start_b)
        top = jnp.maximum(top, jnp.where(earlier, part, -1.0))
        weight = jnp.exp2(part * (TEMP * math.log2(math.e)))
        masked = weight * allowed[:, at : at + LANES]
        if diagonal:
            masked = jnp.where(pos == pos_b, weight, masked)
        weights.append(masked.astype(jnp.bfloat16))
    acc = acc + jnp.dot(
        jnp.concatenate(weights, axis=1), keys, preferred_element_type=jnp.float32
    )
    return acc, top


def column_parts(top):
    rest = jnp.max(top, axis=1, keepdims=True)
    lane = lax.broadcasted_iota(jnp.int32, top.shape, 1)
    out = jnp.zeros(top.shape, jnp.float32)
    for i in range(3):
        part = rest.astype(jnp.bfloat16).astype(jnp.float32)
        out = jnp.where(lane == i, part, out)
        rest = rest - part
    return out


def fold(rows, width, state, out_ref, query, info, feat, blocks, ends, clusters, diagonal=False):
    acc, top = state[:, :width], state[:, width:]
    for i, (keys, pos) in enumerate(blocks):
        acc, top = attend(
            rows, query, info[0], info[1], feat, acc, top, keys, pos, ends, clusters,
            diagonal and i == 0,
        )
    if out_ref.dtype == jnp.bfloat16:
        top = column_parts(top)
    out_ref[:, :width] = acc.astype(out_ref.dtype)
    out_ref[:, width:] = top.astype(out_ref.dtype)


def first_body(rows, width, clusters, len_ref, mask_hbm, a_ref, b_ref, sa_ref, sb_ref,
               f_ref, g_ref, own_ref, sib_ref, info_ref, feat_ref, ends_ref, mask_ref, sem):
    fetch = pltpu.make_async_copy(mask_hbm, mask_ref, sem.at[0])
    fetch.start()
    ends = ends_of(len_ref, clusters)
    own = positions_of(a_ref)
    sib = positions_of(sa_ref)
    pos = jnp.concatenate([column(r) for r in own + sib], axis=0)
    index, start = cluster_parts(pos, ends, clusters)
    count = mask_ref.shape[0]
    block = jnp.floor(pos * (1.0 / rows)).astype(jnp.int32)
    total = pos.shape[0]
    onehot = (block == lax.broadcasted_iota(jnp.int32, (total, count), 1)).astype(jnp.bfloat16)
    wide = count * clusters
    spread = (
        lax.broadcasted_iota(jnp.int32, (count, wide), 1) // clusters
        == lax.broadcasted_iota(jnp.int32, (count, wide), 0)
    ).astype(jnp.bfloat16)
    fetch.wait()
    picked = jnp.dot(
        onehot, mask_ref[...].astype(jnp.bfloat16), preferred_element_type=jnp.float32
    ).astype(jnp.bfloat16)
    picked = jnp.dot(picked, spread, preferred_element_type=jnp.float32)
    lane_cluster = lax.broadcasted_iota(jnp.int32, (total, wide), 1) % clusters
    feat = jnp.where(lane_cluster == index, picked, 0.0).astype(jnp.bfloat16)
    feat_ref[...] = feat
    info_ref[0] = jnp.broadcast_to(pos, (total, LANES))
    info_ref[1] = jnp.broadcast_to(start, (total, LANES))
    keys = jnp.concatenate([rows_of(r, width) for r in (a_ref, b_ref)], axis=0)
    blocks = [(keys, jnp.concatenate(own, axis=1))]
    blocks += gather_keys((f_ref, g_ref), ((0, 0, 1, 1),), width)
    state = jnp.concatenate(
        [jnp.zeros((rows, width), jnp.float32), jnp.full((rows, LANES), -1.0, jnp.float32)],
        axis=1,
    )
    ends_ref[...] = jnp.concatenate(
        [jnp.full((1, rows), e, jnp.float32) for e in ends]
        + [jnp.zeros((ends_ref.shape[0] - len(ends), rows), jnp.float32)],
        axis=0,
    )
    fold(rows, width, state, own_ref, keys, info_ref[:, :rows], feat[:rows], blocks, ends,
         clusters, True)
    other = jnp.concatenate([rows_of(r, width) for r in (sa_ref, sb_ref)], axis=0)
    fold(rows, width, state, sib_ref, other, info_ref[:, rows:], feat[rows:], blocks, ends,
         clusters)


def gather_keys(key_refs, groups, width):
    out = []
    for group in groups:
        first, second = [rows_of(key_refs[r], width) for r in group[::2]]
        pos = [jnp.concatenate(positions_of(key_refs[p]), axis=1) for p in group[1::2]]
        lane = lax.broadcasted_iota(jnp.int32, pos[0].shape, 1)
        out.append((
            jnp.concatenate([first, second], axis=0),
            jnp.where(lane < first.shape[0], pos[0], pos[1]),
        ))
    return out


def middle_body(rows, width, clusters, groups, ends_ref, info_ref, feat_ref, a_ref, b_ref, sa_ref,
                sb_ref, own_in, sib_in, *refs):
    key_refs, (own_ref, sib_ref) = refs[:-2], refs[-2:]
    ends = [ends_ref[c : c + 1, :] for c in range(clusters - 1)]
    blocks = gather_keys(key_refs, groups, width)
    for i, state_in, state_out, pair in (
        (0, own_in, own_ref, (a_ref, b_ref)), (1, sib_in, sib_ref, (sa_ref, sb_ref))
    ):
        query = jnp.concatenate([rows_of(r, width) for r in pair], axis=0)
        part = slice(i * rows, (i + 1) * rows)
        fold(rows, width, state_in[...], state_out, query, info_ref[:, part], feat_ref[part],
             blocks, ends, clusters)


def late_body(rows, width, clusters, ends_ref, info_ref, feat_ref, a_ref, b_ref, own_in, *refs):
    key_refs, own_ref = refs[:-1], refs[-1]
    ends = [ends_ref[c : c + 1, :] for c in range(clusters - 1)]
    blocks = gather_keys(key_refs, ((0, 0, 1, 1),), width)
    query = jnp.concatenate([rows_of(r, width) for r in (a_ref, b_ref)], axis=0)
    fold(rows, width, own_in[...], own_ref, query, info_ref[:, :rows], feat_ref[:rows],
         blocks, ends, clusters)


def join_body(state_ref, f_ref, out_ref):
    rows, wide = state_ref.shape
    panels = wide // LANES
    for i in range(panels):
        out_ref[i * rows : (i + 1) * rows] = state_ref[:, i * LANES : (i + 1) * LANES]
    out_ref[panels * rows : panels * rows + f_ref.shape[0]] = f_ref[...]


def last_body(rows, width, clusters, ends_ref, info_ref, feat_ref, a_ref, b_ref, own_in, got_ref,
              far_ref, dir_ref, out_top):
    ends = [ends_ref[c : c + 1, :] for c in range(clusters - 1)]
    query = jnp.concatenate([rows_of(r, width) for r in (a_ref, b_ref)], axis=0)
    panels = width // LANES
    parts = [got_ref[i * rows : (i + 1) * rows].astype(jnp.float32) for i in range(panels + 1)]
    acc = own_in[:, :width] + jnp.concatenate(parts[:panels], axis=1)
    top = jnp.maximum(own_in[:, width:], jnp.sum(parts[panels], axis=1, keepdims=True))
    key_refs = [got_ref.at[pl.ds((panels + 1) * rows, a_ref.shape[0])], far_ref]
    for keys, pos in gather_keys(key_refs, ((0, 0, 1, 1),), width):
        acc, top = attend(
            rows, query, info_ref[0, :rows], info_ref[1, :rows], feat_ref[:rows], acc, top, keys,
            pos, ends, clusters, False,
        )
    scale = math.sqrt(width) * lax.rsqrt(jnp.sum(acc * acc, axis=1, keepdims=True) + EPS)
    dir_ref[...] = (acc * scale).astype(jnp.bfloat16)
    half = rows // 2
    best = jnp.max(top, axis=1, keepdims=True)
    eye = lax.broadcasted_iota(jnp.int32, (half, half), 0) == lax.broadcasted_iota(
        jnp.int32, (half, half), 1
    )
    lines = [
        jnp.max(jnp.where(eye, best[at : at + half], -1.0), axis=0, keepdims=True)
        for at in (0, half)
    ]
    out_top[...] = jnp.concatenate(lines, axis=0)


def in_hbm(x):
    return pltpu.with_memory_space_constraint(x, pltpu.HBM)


def after(x, *before):
    return lax.optimization_barrier((x, *before))[0]


def per_device(embeddings, dest_pos, cluster_lengths, block_mask):
    rows, width = embeddings.shape
    half = rows // 2
    count = lax.axis_size("blk")
    clusters = cluster_lengths.shape[0]
    steps = count // 4
    ahead, back = ring_perm(count, -1), ring_perm(count, 1)
    sibling = [(i, i ^ 1) for i in range(count)]

    def move(x, perm):
        return lax.ppermute(x, "blk", perm)

    def bf(n, w=width):
        return jax.ShapeDtypeStruct((n, w), jnp.bfloat16)

    def f32(*s):
        return jax.ShapeDtypeStruct(s, jnp.float32)

    sizes = (rows // 2, rows - rows // 2)
    alone = [width // LANES * n for n in sizes]
    full = alone[0] + TAIL
    wide = width + LANES
    state = f32(rows, wide)
    a, b, ah, bh = call(
        functools.partial(prep_body, sizes),
        [bf(n + TAIL, LANES) for n in alone] + [bf(n, LANES) for n in alone], [HB, HB],
        scratch=[
            pltpu.VMEM((rows, width), jnp.float32), pltpu.VMEM((2, half), jnp.int32),
            pltpu.SemaphoreType.DMA((3,)),
        ],
    )(in_hbm(embeddings), in_hbm(dest_pos.reshape(2, half)))

    lead = [(move(a, ahead), move(b, back))]
    follow = [(move(bh, ahead), move(ah, back))]
    sa, sb = move(a, sibling), move(b, sibling)
    work = 8 * rows * rows * width * WEIGHT
    own, sib, info, feat, ends = call(
        functools.partial(first_body, rows, width, clusters),
        [state, state, f32(2, 2 * rows, LANES), bf(2 * rows, count * clusters),
         f32(-(-clusters // 8) * 8, rows)],
        [SM, HB] + [VM] * 6, work,
        scratch=[pltpu.VMEM(block_mask.shape, jnp.int32), pltpu.SemaphoreType.DMA((1,))],
    )(cluster_lengths, block_mask, a, b, sa, sb, *lead[0])

    def middle(own, sib, keys, groups, work, sent=state):
        return call(
            functools.partial(middle_body, rows, width, clusters, groups), [state, sent],
            [VM] * (9 + len(keys)), work, aliases={7: 0, 8: 1} if sent is state else {7: 0},
        )(ends, info, feat, a, b, sa, sb, own, sib, *keys)

    both = (0, 0, 1, 1)
    for step in range(1, steps):
        f, g = lead[-1]
        lead.append((move(f, ahead), move(g, back)))
        if step > 1:
            own, sib = middle(
                own, sib, (*lead[-2], *follow[-2], *lead[-3]), ((3, 5, 2, 4), both),
                work,
            )
        if step < steps - 1:
            f, g = follow[-1]
            follow.append((move(after(f, own), ahead), move(after(g, own), back)))
    own, sib = middle(own, sib, (*lead[-2], *follow[-1]), ((3, 1, 2, 0),), 1,
                      bf(rows, wide))
    stacked = wide // LANES * rows + -(-full // 16) * 16
    joined = call(join_body, [bf(stacked, LANES)], [VM, VM])(sib, lead[-1][0])[0]
    got = move(joined, sibling)
    far = move(after(lead[-1][1], own), sibling)
    shared = (ends, info, feat, a, b)
    own = call(
        functools.partial(late_body, rows, width, clusters), [state], [VM] * 8, work, aliases={5: 0},
    )(*shared, own, *lead[-1])[0]
    out_dir, out_top = call(
        functools.partial(last_body, rows, width, clusters),
        [bf(rows), f32(2, half)], [VM] * 8,
    )(*shared, own, got, far)
    return out_top.reshape(rows), out_dir


def solution(mesh):
    placed = (P(("groups", "blk"), None), P(("groups", "blk")), P("groups"), P("groups", None))
    return jax.shard_map(
        per_device,
        mesh=mesh,
        in_specs=placed,
        out_specs=(P(("groups", "blk")), P(("groups", "blk"), None)),
        check_vma=False,
    )
```
